256 devices in a mesh: wide: 16 (over z_hi, y), narrow: 16 (over z_lo, x, core).
Axes of the slice: x: 4, y: 4, z: 8 (z_hi: 4, z_lo: 2; z = z_hi * 2 + z_lo), core: 2. Of those that a mesh axis runs over, the one named last changes fastest.
Arguments:
- points: bfloat16 [65536, 768], P(('wide', 'narrow')), may hold values from -2 to 2
- centroids: bfloat16 [16384, 768], P('narrow'), may hold values from -1 to 1
Outputs:
- new_centroids: bfloat16 [16384, 768], P('narrow')
- counts: float32 [16384], P('narrow')
The draws below stay inside these ranges and needn't reach their ends.
All inputs are finite; a program needn't handle non-finite values.
Results may differ from the reference program's by a relative error of at most 0.0036.
Values may be sent and summed in bfloat16 or wider, within the bound.
A program may use at most 128 MiB of HBM per device.

```python
import math
import jax
import jax.numpy as jnp
from jax import lax

D = 768
K = 16384
POINTS = 65536


def shared_centres(key):
    return jax.random.normal(key, (K, D), jnp.float32) / math.sqrt(D)


def draw_centroids(key, part):
    base = shared_centres(key)
    return jnp.clip(base, -1.0, 1.0).astype(jnp.bfloat16)


def draw_points(key, part):
    key = jax.random.fold_in(key, 23)
    second = jax.random.fold_in(key, 1)
    values = jnp.clip(jax.random.normal(second, (POINTS, D), jnp.float32) * 0.05, -0.3, 0.3)
    return jnp.clip(values, -2.0, 2.0).astype(jnp.bfloat16)


def setup_inputs(seed: int = 0) -> dict:
    streams_of = jax.random.split(jax.random.key(seed), 3)
    return {
        "points": draw_points(jax.random.fold_in(streams_of[2], 71), 0),
        "centroids": draw_centroids(jax.random.fold_in(streams_of[2], 71), 0),
    }


def reference(points, centroids):
    block = min(2048, POINTS)
    steps = POINTS // block
    blocks = points.reshape(steps, block, D)
    cent = centroids.astype(jnp.float32)

    def visit(carry, rows):
        sums, counts = carry
        logits = 60.0 * jnp.dot(rows.astype(jnp.float32), cent.T, preferred_element_type=jnp.float32)
        row_max = lax.optimization_barrier(jnp.max(logits, axis=1, keepdims=True))
        expo = jnp.exp(logits - row_max)
        resp = (expo / lax.optimization_barrier(jnp.sum(expo, axis=1, keepdims=True))).astype(jnp.bfloat16)
        sums = sums + jnp.dot(resp.astype(jnp.float32).T, rows.astype(jnp.float32), preferred_element_type=jnp.float32)
        counts = counts + lax.optimization_barrier(jnp.sum(resp.astype(jnp.float32), axis=0))
        return ((sums, counts), None)
    start = (jnp.zeros((K, D), jnp.float32), jnp.zeros((K,), jnp.float32))
    (sums, counts), _ = lax.scan(visit, start, blocks)
    scale = lax.rsqrt(lax.optimization_barrier(jnp.sum(sums * sums, axis=1, keepdims=True)) + 1e-06)
    return ((sums * scale).astype(jnp.bfloat16), counts)
```

```python
import functools

import jax
import jax.numpy as jnp
from jax import lax
from jax.experimental import pallas as pl
from jax.experimental.pallas import tpu as pltpu
from jax.sharding import PartitionSpec as P

MESH = pl.DeviceIdType.MESH
F32 = jnp.float32
BF16 = jnp.bfloat16
D = 768
NS = 4
R = 128 // NS
G = 8 * R
KB = 256
RATE = 60.0 * 1.4426950408889634


def kernel(
    pts_in, cen_in, out_ref, cnt_out,
    pts, cen, e, m_tile, t_tile, s_tile, st_send, st_recv, z2_send, z2_recv,
    acc, cacc, yb, ry2, rym, zb, rz, outv, cnt, cnt_y, cnt_z,
    g_send, g_recv, loc_sem, st_ss, st_rs, z2_ss, z2_rs,
    ry_ss, ry_rs, rz_ss, rz_rs, az_ss, az_rs, ay_ss, ay_rs, c_ss, c_rs, io_sem,
):
    wide, narrow = lax.axis_index("wide"), lax.axis_index("narrow")
    h, y = wide // 4, wide % 4
    zl, x, c = narrow // 8, (narrow // 2) % 4, narrow % 2
    z = 2 * h + zl
    xm, xp, x2 = (x + 3) % 4, (x + 1) % 4, (x + 2) % 4

    def at(dx=0, dy=0, dz=0, dc=0):
        zz = (z + dz + 8) % 8
        return (
            (zz // 2) * 4 + (y + dy + 4) % 4,
            (zz % 2) * 8 + ((x + dx + 4) % 4) * 2 + (c + dc) % 2,
        )

    def send(src, dst, ss, rs, device):
        return pltpu.make_async_remote_copy(
            src_ref=src, dst_ref=dst, send_sem=ss, recv_sem=rs, device_id=device, device_id_type=MESH
        )

    mates = [(d // 2, d % 2) for d in range(1, 8)]
    cen_copy = pltpu.make_async_copy(cen_in, cen, io_sem.at[0])
    cen_copy.start()

    partners = [at(dx=a, dc=b) for a, b in mates]
    partners += [at(dz=1), at(dz=-1), at(dy=1), at(dy=2), at(dy=3), at(dz=2), at(dz=4), at(dz=6)]
    barrier = pltpu.get_barrier_semaphore()
    for device in partners:
        pl.semaphore_signal(barrier, inc=1, device_id=device, device_id_type=MESH)
    pl.semaphore_wait(barrier, len(partners))

    def own(i):
        return pts_in.at[:, pl.ds(i * R, R)]

    def gcopy(i, n):
        ss, rs = g_send.at[i, n], g_recv.at[i, n]
        if n == 0:
            return send(own(i), pts.at[i, pl.ds(0, 2), x, c], ss, rs, at(dx=1))
        if n == 1:
            return send(own(i), pts.at[i, pl.ds(0, 2), x, c], ss, rs, at(dx=-1))
        if n == 2:
            return send(pts.at[i, 0, xm, c], pts.at[i, 0, xm, c], ss, rs, at(dx=1))
        if n == 3:
            return send(pts.at[i, 1, xp, c], pts.at[i, 1, xp, c], ss, rs, at(dx=-1))
        if n == 4:
            return send(pts_in.at[0, pl.ds(i * R, R)], pts.at[i, 2, x, c], ss, rs, at(dz=1))
        if n == 5:
            return send(pts_in.at[1, pl.ds(i * R, R)], pts.at[i, 3, x, c], ss, rs, at(dz=-1))
        if n in (6, 8, 10):
            o = {6: xm, 8: xp, 10: x2}[n]
            return send(pts.at[i, 0, o, c], pts.at[i, 2, o, c], ss, rs, at(dz=1))
        if n in (7, 9, 11):
            o = {7: xm, 9: xp, 11: x2}[n]
            return send(pts.at[i, 1, o, c], pts.at[i, 3, o, c], ss, rs, at(dz=-1))
        if n == 12:
            half = pts.at[i, pl.ds(0, 2), :, c]
        else:
            half = pts.at[i, n - 11, :, c]
        return send(half, half, ss, rs, at(dc=1))

    def local(i):
        return pltpu.make_async_copy(own(i), pts.at[i, pl.ds(0, 2), x, c], loc_sem.at[i])

    def start(i, *ns):
        for n in ns:
            gcopy(i, n).start()

    def arrived(i, *ns):
        for n in ns:
            gcopy(i, n).wait_recv()

    def ev0(i):
        start(i, 0, 1, 4, 5)
        local(i).start()

    def ev1(i):
        arrived(i, 0, 1)
        start(i, 2, 3, 6, 7, 8, 9)

        @pl.when(i + 1 < NS)
        def _():
            ev0(i + 1)

    def ev2(i):
        arrived(i, 2, 3)
        start(i, 10, 11)
        local(i).wait()
        start(i, 12)

    def ev3(i):
        arrived(i, 4, 6, 8, 10)
        start(i, 13)
        arrived(i, 5, 7, 9, 11)
        start(i, 14)

    def mm1(i, g):
        p = pts[i, g].reshape(G, D)
        for k in range(4):
            l = lax.dot_general(
                cen[k * KB : (k + 1) * KB, :], p, (((1,), (1,)), ((), ())), preferred_element_type=F32
            )
            m = jnp.max(l, axis=0, keepdims=True)
            v = jnp.exp2((l - m) * RATE)
            e[i, g, k * KB : (k + 1) * KB, :] = v
            t = jnp.sum(v, axis=0, keepdims=True)
            for j in range(2):
                m_tile[i, k, 2 * g + j : 2 * g + j + 1, :] = m[:, j * 128 : (j + 1) * 128]
                t_tile[i, k, 2 * g + j : 2 * g + j + 1, :] = t[:, j * 128 : (j + 1) * 128]

    def st_copy(i, d):
        a, b = mates[d]
        return send(st_send.at[i], st_recv.at[i, d], st_ss.at[i, d], st_rs.at[i, d], at(dx=a, dc=b))

    def z2_copy(i, d):
        return send(z2_send.at[i], z2_recv.at[i, d], z2_ss.at[i, d], z2_rs.at[i, d], at(dz=1 - 2 * d))

    def merge(parts):
        m = functools.reduce(jnp.maximum, [a for a, _ in parts])
        return m, sum(t * jnp.exp2((a - m) * RATE) for a, t in parts)

    def st1(i):
        m, t = merge([(m_tile[i, k], t_tile[i, k]) for k in range(4)])
        st_send[i, 0] = m
        st_send[i, 1] = t
        for d in range(7):
            st_copy(i, d).start()

    def st2(i):
        for d in range(7):
            st_copy(i, d).wait_recv()
        parts = [(st_send[i, 0], st_send[i, 1])]
        parts += [(st_recv[i, d, 0], st_recv[i, d, 1]) for d in range(7)]
        m, t = merge(parts)
        z2_send[i, 0] = m
        z2_send[i, 1] = t
        for d in range(2):
            z2_copy(i, d).start()

    def st3(i):
        for d in range(2):
            z2_copy(i, d).wait_recv()
        row = lax.broadcasted_iota(jnp.int32, (8, 128), 0)
        above = (row < 2) | (row >= 6)

        def other(n):
            lo, hi = z2_recv[i, 0, n], z2_recv[i, 1, n]
            turn = lambda a: jnp.concatenate([a[4:], a[:4]], axis=0)
            return jnp.where(above, turn(hi), turn(lo))

        m, t = merge([(z2_send[i, 0], z2_send[i, 1]), (other(0), other(1))])
        inv = 1.0 / t
        for k in range(4):
            s_tile[i, k] = jnp.exp2((m_tile[i, k] - m) * RATE) * inv

    ev0(0)
    ev1(0)
    ev2(0)
    cen_copy.wait()
    arrived(0, 12)

    def step(i, carry):
        @pl.when(i < NS)
        def _():
            mm1(i, 0)

        @pl.when(i > 0)
        def _():
            ev3(i - 1)

        @pl.when(i + 1 < NS)
        def _():
            ev1(i + 1)

        @pl.when(i < NS)
        def _():
            mm1(i, 1)

        @pl.when(i > 0)
        def _():
            arrived(i - 1, 13, 14)
            mm1(i - 1, 2)

        @pl.when(i + 1 < NS)
        def _():
            ev2(i + 1)

        @pl.when(i > 0)
        def _():
            mm1(i - 1, 3)
            st1(i - 1)

        @pl.when(i > 1)
        def _():
            st2(i - 2)

        @pl.when(i + 1 < NS)
        def _():
            arrived(i + 1, 12)

        return carry

    lax.fori_loop(0, NS + 1, step, 0)

    deltas = (2, 1, 3, 0)

    def mm2(n, lo, hi):
        b = (h + deltas[n]) % 4
        r0 = pl.multiple_of(b * KB, KB)

        def part(i, carry):
            cs = jnp.zeros((KB, 128), F32)
            resp = []
            for g in range(4):
                for j in range(2):
                    v = e[i, g, pl.ds(r0, KB), j * 128 : (j + 1) * 128] * s_tile[i, b, 2 * g + j : 2 * g + j + 1, :]
                    cs = cs + v
                    resp.append(v.astype(BF16))
            cacc[pl.ds(r0, KB), :] += cs
            acc[n] += jnp.dot(
                jnp.concatenate(resp, axis=1), pts[i].reshape(4 * G, D), preferred_element_type=F32
            )
            return carry

        lax.fori_loop(lo, hi, part, 0)

    ym, yp, y2 = (y + 3) % 4, (y + 1) % 4, (y + 2) % 4

    def half(ref, owner, side):
        return ref.at[pl.ds(pl.multiple_of(owner * 64 + side * 32, 32), 32)]

    def ycopy(n, q):
        up, kind = q % 2 == 0, q // 2
        ss, rs = ry_ss.at[n, q], ry_rs.at[n, q]
        to = at(dy=1 if up else -1)
        near = yp if up else ym
        side = 0 if up else 1
        if kind == 0:
            return send(half(yb.at[n], y2, side), ry2.at[n, side], ss, rs, to)
        if kind == 1:
            return send(half(yb.at[n], near, 1 - side), rym.at[n, side, pl.ds((1 - side) * 32, 32)], ss, rs, to)
        return send(half(yb.at[n], near, side), rym.at[n, side, pl.ds(side * 32, 32)], ss, rs, to)

    def rs_a(n):
        yb[n] = acc[n].astype(BF16)
        for q in range(4):
            ycopy(n, q).start()

    def rs_b(n):
        for side, near in ((0, yp), (1, ym)):
            ycopy(n, side).wait_recv()
            rows = pl.ds(pl.multiple_of(near * 64 + side * 32, 32), 32)
            yb[n, rows] = (acc[n, rows] + ry2[n, side].astype(F32)).astype(BF16)
            ycopy(n, 4 + side).start()

    def zcopy(n):
        return send(zb.at[n], rz.at[n], rz_ss.at[n], rz_rs.at[n], at(dz=2 * deltas[n]))

    def rs_c(n):
        for q in range(2, 6):
            ycopy(n, q).wait_recv()
        total = acc[n, pl.ds(pl.multiple_of(y * 64, 64), 64)]
        total = total + rym[n, 0].astype(F32) + rym[n, 1].astype(F32)
        if n < 3:
            zb[n] = total.astype(BF16)
            zcopy(n).start()
        return total

    acc[...] = jnp.zeros_like(acc)
    cacc[...] = jnp.zeros_like(cacc)
    for i in range(NS - 1):
        st3(i)
    st2(NS - 1)
    mm2(0, 0, NS - 1)
    st3(NS - 1)
    mm2(0, NS - 1, NS)
    rs_a(0)
    mm2(1, 0, NS)
    rs_a(1)
    rs_b(0)
    mm2(2, 0, NS)
    rs_a(2)
    rs_b(1)
    rs_c(0)
    mm2(3, 0, NS)
    rs_a(3)
    rs_b(2)
    rs_c(1)

    rest, wide_cnt = cacc[...], jnp.zeros((8, 1024), F32)
    ones = jnp.ones((8, 128), BF16)
    for _ in range(3):
        term = rest.astype(BF16)
        wide_cnt += lax.dot_general(ones, term, (((1,), (1,)), ((), ())), preferred_element_type=F32)
        rest = rest - term.astype(F32)
    row = lax.broadcasted_iota(jnp.int32, (8, 128), 0)
    dense = jnp.zeros((8, 128), F32)
    for r in range(8):
        dense = jnp.where(row == r, wide_cnt[:, r * 128 : (r + 1) * 128], dense)
    cnt[0] = dense

    def ccopy(n):
        d = n % 3 + 1
        if n < 3:
            return send(cnt.at[0], cnt_y.at[d - 1], c_ss.at[n], c_rs.at[n], at(dy=d))
        return send(cnt.at[1], cnt_z.at[d - 1], c_ss.at[n], c_rs.at[n], at(dz=2 * d))

    for n in range(3):
        ccopy(n).start()
    rs_b(3)
    rs_c(2)
    total = rs_c(3)
    for n in range(3):
        ccopy(n).wait_recv()
    cnt[1] = cnt[0] + cnt_y[0] + cnt_y[1] + cnt_y[2]
    for n in range(3, 6):
        ccopy(n).start()
    for n in range(3):
        zcopy(n).wait_recv()
        total = total + rz[n].astype(F32)

    scale = lax.rsqrt(jnp.sum(total * total, axis=1, keepdims=True) + 1e-06)
    outv[h, y] = (total * scale).astype(BF16)

    def azcopy(d):
        return send(outv.at[h, y], outv.at[h, y], az_ss.at[d], az_rs.at[d], at(dz=2 * d))

    def aycopy(b, n, q):
        up, forward = q % 2 == 0, q >= 2
        to, ss, rs = at(dy=1 if up else -1), ay_ss.at[n, q], ay_rs.at[n, q]
        if not forward:
            return send(outv.at[b, y], outv.at[b, y], ss, rs, to)
        block = outv.at[b, ym if up else yp, pl.ds(0 if up else 32, 32)]
        return send(block, block, ss, rs, to)

    order = (0, 1, 3, 2)
    for d in (1, 3, 2):
        azcopy(d).start()

    def ag_a(n):
        d = order[n]
        if d:
            azcopy(d).wait_recv()
        for q in range(2):
            aycopy((h - d + 4) % 4, n, q).start()

    def ag_b(n):
        b = (h - order[n] + 4) % 4
        for q in range(2):
            aycopy(b, n, q).wait_recv()
            aycopy(b, n, 2 + q).start()

    def writeback(n):
        b = (h - order[n] + 4) % 4
        return pltpu.make_async_copy(outv.at[b], out_ref.at[b], io_sem.at[1 + n])

    def ag_c(n):
        b = (h - order[n] + 4) % 4
        for q in range(2, 4):
            aycopy(b, n, q).wait_recv()
        writeback(n).start()

    ag_a(0)
    ag_a(1)
    ag_b(0)
    ag_a(2)
    ag_b(1)
    ag_c(0)
    ag_a(3)
    ag_b(2)
    ag_c(1)
    ag_b(3)
    ag_c(2)
    for n in range(3, 6):
        ccopy(n).wait_recv()
    cnt_out[...] = cnt[1] + cnt_z[0] + cnt_z[1] + cnt_z[2]
    ag_c(3)

    def sent(i, carry):
        for n in range(15):
            gcopy(i, n).wait_send()
        for d in range(7):
            st_copy(i, d).wait_send()
        for d in range(2):
            z2_copy(i, d).wait_send()
        return carry

    lax.fori_loop(0, NS, sent, 0)
    for n in range(4):
        for q in range(6):
            ycopy(n, q).wait_send()
        b = (h - order[n] + 4) % 4
        for q in range(4):
            aycopy(b, n, q).wait_send()
    for n in range(3):
        zcopy(n).wait_send()
        azcopy(n + 1).wait_send()
    for n in range(6):
        ccopy(n).wait_send()
    for n in range(4):
        writeback(n).wait()


def on_device(points, centroids):
    dma = pltpu.SemaphoreType.DMA
    out, counts = pl.pallas_call(
        kernel,
        out_shape=(
            jax.ShapeDtypeStruct((4, 4, 64, D), BF16),
            jax.ShapeDtypeStruct((8, 128), F32),
        ),
        in_specs=[pl.BlockSpec(memory_space=pl.ANY)] * 2,
        out_specs=(
            pl.BlockSpec(memory_space=pl.ANY),
            pl.BlockSpec(memory_space=pltpu.VMEM),
        ),
        scratch_shapes=[
            pltpu.VMEM((NS, 4, 4, 2, R, D), BF16),
            pltpu.VMEM((1024, D), BF16),
            pltpu.VMEM((NS, 4, 1024, G), F32),
            pltpu.VMEM((NS, 4, 8, 128), F32),
            pltpu.VMEM((NS, 4, 8, 128), F32),
            pltpu.VMEM((NS, 4, 8, 128), F32),
            pltpu.VMEM((NS, 2, 8, 128), F32),
            pltpu.VMEM((NS, 7, 2, 8, 128), F32),
            pltpu.VMEM((NS, 2, 8, 128), F32),
            pltpu.VMEM((NS, 2, 2, 8, 128), F32),
            pltpu.VMEM((4, KB, D), F32),
            pltpu.VMEM((1024, 128), F32),
            pltpu.VMEM((4, KB, D), BF16),
            pltpu.VMEM((4, 2, 32, D), BF16),
            pltpu.VMEM((4, 2, 64, D), BF16),
            pltpu.VMEM((3, 64, D), BF16),
            pltpu.VMEM((3, 64, D), BF16),
            pltpu.VMEM((4, 4, 64, D), BF16),
            pltpu.VMEM((2, 8, 128), F32),
            pltpu.VMEM((3, 8, 128), F32),
            pltpu.VMEM((3, 8, 128), F32),
            dma((NS, 15)), dma((NS, 15)), dma((NS,)),
            dma((NS, 7)), dma((NS, 7)), dma((NS, 2)), dma((NS, 2)),
            dma((4, 6)), dma((4, 6)), dma((3,)), dma((3,)),
            dma((4,)), dma((4,)), dma((4, 4)), dma((4, 4)),
            dma((6,)), dma((6,)), dma((5,)),
        ],
        compiler_params=pltpu.CompilerParams(
            collective_id=0, has_side_effects=True, vmem_limit_bytes=56 << 20
        ),
        cost_estimate=pl.CostEstimate(
            flops=4 * 4096 * 1024 * D, bytes_accessed=4 << 20, transcendentals=4096 * 1024
        ),
    )(points.reshape(2, 128, D), centroids)
    return out.reshape(1024, D), counts.reshape(1024)


def solution(mesh):
    placed = (P(("wide", "narrow"), None), P("narrow", None))
    return jax.shard_map(
        on_device,
        mesh=mesh,
        in_specs=placed,
        out_specs=(P("narrow", None), P("narrow")),
        check_vma=False,
    )
```

```python
import functools

import jax
import jax.numpy as jnp
from jax import lax
from jax.experimental import pallas as pl
from jax.experimental.pallas import tpu as pltpu
from jax.sharding import PartitionSpec as P

MESH = pl.DeviceIdType.MESH
F32 = jnp.float32
BF16 = jnp.bfloat16
D = 768
NS = 4
R = 128 // NS
G = 8 * R
KB = 256
RATE = 60.0 * 1.4426950408889634


def kernel(
    pts_in, cen_in, out_ref, cnt_out,
    pts, cen, e, m_tile, t_tile, s_tile, st_send, st_recv, z2_send, z2_recv,
    acc, cacc, yb, ry2, rym, zt, zb, rz, outv, cnt, cnt_y, cnt_z,
    g_send, g_recv, loc_sem, st_ss, st_rs, z2_ss, z2_rs,
    y2_ss, y2_rs, ym_ss, ym_rs, rz_ss, rz_rs, az_ss, az_rs, ay_ss, ay_rs, c_ss, c_rs, io_sem,
):
    wide, narrow = lax.axis_index("wide"), lax.axis_index("narrow")
    h, y = wide // 4, wide % 4
    zl, x, c = narrow // 8, (narrow // 2) % 4, narrow % 2
    z = 2 * h + zl
    xm, xp, x2 = (x + 3) % 4, (x + 1) % 4, (x + 2) % 4
    ym, yp, y2 = (y + 3) % 4, (y + 1) % 4, (y + 2) % 4

    def at(dx=0, dy=0, dz=0, dc=0):
        zz = (z + dz + 8) % 8
        return (
            (zz // 2) * 4 + (y + dy + 4) % 4,
            (zz % 2) * 8 + ((x + dx + 4) % 4) * 2 + (c + dc) % 2,
        )

    def send(src, dst, ss, rs, device):
        return pltpu.make_async_remote_copy(
            src_ref=src, dst_ref=dst, send_sem=ss, recv_sem=rs, device_id=device, device_id_type=MESH
        )

    def wait(ref, sem):
        send(ref, ref, sem, sem, at(dc=1)).wait_recv()

    mates = [(d // 2, d % 2) for d in range(1, 8)]
    cen_copy = pltpu.make_async_copy(cen_in, cen, io_sem.at[0])
    cen_copy.start()

    partners = [at(dx=a, dc=b) for a, b in mates]
    partners += [at(dz=1), at(dz=-1), at(dy=1), at(dy=2), at(dy=3), at(dz=2), at(dz=4), at(dz=6)]
    barrier = pltpu.get_barrier_semaphore()
    for device in partners:
        pl.semaphore_signal(barrier, inc=1, device_id=device, device_id_type=MESH)
    acc[...] = jnp.zeros_like(acc)
    cacc[...] = jnp.zeros_like(cacc)
    pl.semaphore_wait(barrier, len(partners))

    def own(i):
        return pts_in.at[:, pl.ds(i * R, R)]

    def gcopy(i, n):
        q = n if n < 4 else n - 6 if n >= 12 else 4 + n % 2
        ss, rs = g_send.at[q], g_recv.at[i, q]
        if n == 0:
            return send(own(i), pts.at[i, pl.ds(0, 2), x, c], ss, rs, at(dx=1))
        if n == 1:
            return send(own(i), pts.at[i, pl.ds(0, 2), x, c], ss, rs, at(dx=-1))
        if n == 2:
            return send(pts.at[i, 0, xm, c], pts.at[i, 0, xm, c], ss, rs, at(dx=1))
        if n == 3:
            return send(pts.at[i, 1, xp, c], pts.at[i, 1, xp, c], ss, rs, at(dx=-1))
        if n == 4:
            return send(pts_in.at[0, pl.ds(i * R, R)], pts.at[i, 2, x, c], ss, rs, at(dz=1))
        if n == 5:
            return send(pts_in.at[1, pl.ds(i * R, R)], pts.at[i, 3, x, c], ss, rs, at(dz=-1))
        if n in (6, 8, 10):
            o = {6: xm, 8: xp, 10: x2}[n]
            return send(pts.at[i, 0, o, c], pts.at[i, 2, o, c], ss, rs, at(dz=1))
        if n in (7, 9, 11):
            o = {7: xm, 9: xp, 11: x2}[n]
            return send(pts.at[i, 1, o, c], pts.at[i, 3, o, c], ss, rs, at(dz=-1))
        if n == 12:
            half = pts.at[i, pl.ds(0, 2), :, c]
        else:
            half = pts.at[i, n - 11, :, c]
        return send(half, half, ss, rs, at(dc=1))

    def local(i):
        return pltpu.make_async_copy(own(i), pts.at[i, pl.ds(0, 2), x, c], loc_sem.at[i])

    def start(i, *ns):
        for n in ns:
            gcopy(i, n).start()

    def arrived(i, *ns):
        for n in ns:
            gcopy(i, n).wait_recv()

    def ev0(i):
        start(i, 0, 1, 4, 5)
        local(i).start()

    def ev1(i):
        arrived(i, 0, 1)
        start(i, 2, 3, 6, 7, 8, 9)

        @pl.when(i + 2 < NS)
        def _():
            ev0(i + 2)

    def ev2(i):
        arrived(i, 2, 3)
        start(i, 10, 11)
        local(i).wait()
        start(i, 12)

    def ev3(i):
        for n in (0, 1):
            wait(pts.at[i, 2 + n, :, c], g_recv.at[i, 4 + n])
            start(i, 13 + n)

    def mm1(i, g):
        p = pts[i, g].reshape(G, D)
        for k in range(4):
            l = lax.dot_general(
                cen[k * KB : (k + 1) * KB, :], p, (((1,), (1,)), ((), ())), preferred_element_type=F32
            )
            m = jnp.max(l, axis=0, keepdims=True)
            v = jnp.exp2((l - m) * RATE)
            e[i, g, k * KB : (k + 1) * KB, :] = v
            t = jnp.sum(v, axis=0, keepdims=True)
            for j in range(2):
                m_tile[i, k, 2 * g + j : 2 * g + j + 1, :] = m[:, j * 128 : (j + 1) * 128]
                t_tile[i, k, 2 * g + j : 2 * g + j + 1, :] = t[:, j * 128 : (j + 1) * 128]

    def st_copy(i, d):
        a, b = mates[d]
        return send(st_send.at[i], st_recv.at[i, d], st_ss.at[0], st_rs.at[i], at(dx=a, dc=b))

    def z2_copy(i, d):
        return send(z2_send.at[i], z2_recv.at[i, d], z2_ss.at[0], z2_rs.at[i], at(dz=1 - 2 * d))

    def merge(parts):
        m = functools.reduce(jnp.maximum, [a for a, _ in parts])
        return m, sum(t * jnp.exp2((a - m) * RATE) for a, t in parts)

    def st1(i):
        m, t = merge([(m_tile[i, k], t_tile[i, k]) for k in range(4)])
        st_send[i, 0] = m
        st_send[i, 1] = t
        for d in range(7):
            st_copy(i, d).start()

    def st2(i):
        wait(st_recv.at[i], st_rs.at[i])
        parts = [(st_send[i, 0], st_send[i, 1])]
        parts += [(st_recv[i, d, 0], st_recv[i, d, 1]) for d in range(7)]
        m, t = merge(parts)
        z2_send[i, 0] = m
        z2_send[i, 1] = t
        for d in range(2):
            z2_copy(i, d).start()

    def st3(i):
        wait(z2_recv.at[i], z2_rs.at[i])
        row = lax.broadcasted_iota(jnp.int32, (8, 128), 0)
        above = (row < 2) | (row >= 6)

        def other(n):
            lo, hi = z2_recv[i, 0, n], z2_recv[i, 1, n]
            turn = lambda a: jnp.concatenate([a[4:], a[:4]], axis=0)
            return jnp.where(above, turn(hi), turn(lo))

        m, t = merge([(z2_send[i, 0], z2_send[i, 1]), (other(0), other(1))])
        inv = 1.0 / t
        for k in range(4):
            s_tile[i, k] = jnp.exp2((m_tile[i, k] - m) * RATE) * inv

    ev0(0)
    ev0(1)
    ev1(0)
    ev2(0)
    ev1(1)
    cen_copy.wait()
    arrived(0, 12)

    def step(i, carry):
        @pl.when(i < NS)
        def _():
            mm1(i, 0)

        @pl.when(i + 1 < NS)
        def _():
            ev2(i + 1)

        @pl.when(i < NS)
        def _():
            mm1(i, 1)

        @pl.when(i + 2 < NS)
        def _():
            ev1(i + 2)

        @pl.when(i > 1)
        def _():
            st2(i - 2)

        @pl.when(i > 0)
        def _():
            arrived(i - 1, 13, 14)
            mm1(i - 1, 2)
            mm1(i - 1, 3)
            st1(i - 1)

        @pl.when(i < NS)
        def _():
            ev3(i)

        @pl.when(i > 2)
        def _():
            st3(i - 3)

        @pl.when(i + 1 < NS)
        def _():
            arrived(i + 1, 12)

        return carry

    lax.fori_loop(0, NS + 1, step, 0)

    def mm2(n, lo, hi):
        def part(i, carry):
            cs = jnp.zeros((KB, 128), F32)
            resp = []
            for g in range(4):
                for j in range(2):
                    v = e[i, g, n * KB : (n + 1) * KB, j * 128 : (j + 1) * 128]
                    v = v * s_tile[i, n, 2 * g + j : 2 * g + j + 1, :]
                    cs = cs + v
                    resp.append(v.astype(BF16))
            cacc[n * KB : (n + 1) * KB, :] += cs
            acc[n] += jnp.dot(
                jnp.concatenate(resp, axis=1), pts[i].reshape(4 * G, D), preferred_element_type=F32
            ).reshape(4, 64, D)
            return carry

        lax.fori_loop(lo, hi, part, 0)

    def cols(side):
        return pl.ds(side * (D // 2), D // 2)

    def ycopy(n, kind, side):
        to, near = at(dy=1 - 2 * side), (yp, ym)[side]
        if kind == 0:
            return send(yb.at[n, y2, :, cols(side)], ry2.at[n, side], y2_ss.at[0], y2_rs.at[n, side], to)
        part = cols(1 - side if kind == 1 else side)
        return send(yb.at[n, near, :, part], rym.at[n, side, :, part], ym_ss.at[0], ym_rs.at[n], to)

    def rs_a(n):
        yb[n] = acc[n].astype(BF16)
        for kind in range(2):
            for side in range(2):
                ycopy(n, kind, side).start()

    def rs_b(n):
        for side, near in ((0, yp), (1, ym)):
            ycopy(n, 0, side).wait_recv()
            part = cols(side)
            yb[n, near, :, part] = (acc[n, near, :, part] + ry2[n, side].astype(F32)).astype(BF16)
            ycopy(n, 2, side).start()

    def zcopy(n, d):
        return send(zb.at[n, (h + d) % 4], rz.at[n, d - 1], rz_ss.at[0], rz_rs.at[n], at(dz=2 * d))

    def rs_c(n):
        wait(rym.at[n], ym_rs.at[n])
        total = acc[n, y] + rym[n, 0].astype(F32) + rym[n, 1].astype(F32)
        zt[n] = total.reshape(4, 16, D)
        zb[n] = total.astype(BF16).reshape(4, 16, D)
        for d in (2, 1, 3):
            zcopy(n, d).start()

    def azcopy(n, d):
        return send(outv.at[n, y, h], outv.at[n, y, h], az_ss.at[0], az_rs.at[n], at(dz=2 * d))

    def aycopy(n, q):
        side = q % 2
        to, ss, rs = at(dy=1 - 2 * side), ay_ss.at[q // 2], ay_rs.at[n, q]
        block = outv.at[n, y] if q < 2 else outv.at[n, (ym, yp)[side], :, :, cols(side)]
        return send(block, block, ss, rs, to)

    def writeback(n):
        return pltpu.make_async_copy(outv.at[n], out_ref.at[n], io_sem.at[1 + n])

    def ag_f(n):
        wait(rz.at[n], rz_rs.at[n])
        total = zt[n, h]
        for d in range(3):
            total = total + rz[n, d].astype(F32)
        scale = lax.rsqrt(jnp.sum(total * total, axis=1, keepdims=True) + 1e-06)
        outv[n, y, h] = (total * scale).astype(BF16)
        for d in (2, 1, 3):
            azcopy(n, d).start()

    def ag_g(n):
        wait(rz.at[n], az_rs.at[n])
        for q in range(2):
            aycopy(n, q).start()

    def ag_h(n):
        for q in range(2):
            aycopy(n, q).wait_recv()
            aycopy(n, 2 + q).start()

    def ag_i(n):
        for q in range(2, 4):
            aycopy(n, q).wait_recv()
        writeback(n).start()

    def ccopy(n):
        d = n % 3 + 1
        if n < 3:
            return send(cnt.at[0], cnt_y.at[d - 1], c_ss.at[0], c_rs.at[0], at(dy=d))
        return send(cnt.at[1], cnt_z.at[d - 1], c_ss.at[1], c_rs.at[1], at(dz=2 * d))

    def cnt_a():
        rest, lanes = cacc[...], jnp.zeros((8, 1024), F32)
        ones = jnp.ones((8, 128), BF16)
        for _ in range(3):
            term = rest.astype(BF16)
            lanes += lax.dot_general(ones, term, (((1,), (1,)), ((), ())), preferred_element_type=F32)
            rest = rest - term.astype(F32)
        row = lax.broadcasted_iota(jnp.int32, (8, 128), 0)
        dense = jnp.zeros((8, 128), F32)
        for r in range(8):
            dense = jnp.where(row == r, lanes[:, r * 128 : (r + 1) * 128], dense)
        cnt[0] = dense
        for n in range(3):
            ccopy(n).start()

    def cnt_b():
        wait(cnt_y, c_rs.at[0])
        cnt[1] = cnt[0] + cnt_y[0] + cnt_y[1] + cnt_y[2]
        for n in range(3, 6):
            ccopy(n).start()

    def cnt_c():
        wait(cnt_z, c_rs.at[1])
        cnt_out[...] = cnt[1] + cnt_z[0] + cnt_z[1] + cnt_z[2]

    mm2(0, 0, NS - 2)
    st3(NS - 2)
    st2(NS - 1)
    mm2(0, NS - 2, NS - 1)
    st3(NS - 1)
    mm2(0, NS - 1, NS)
    rs_a(0)
    mm2(1, 0, NS)
    rs_a(1)
    rs_b(0)
    mm2(2, 0, NS)
    rs_a(2)
    rs_b(1)
    rs_c(0)
    mm2(3, 0, NS)
    rs_a(3)
    rs_b(2)
    rs_c(1)
    ag_f(0)
    rs_b(3)
    rs_c(2)
    cnt_a()
    ag_f(1)
    rs_c(3)
    ag_g(0)
    ag_f(2)
    cnt_b()
    ag_h(0)
    ag_g(1)
    ag_f(3)
    ag_h(1)
    ag_i(0)
    ag_g(2)
    ag_h(2)
    ag_i(1)
    ag_g(3)
    cnt_c()
    ag_h(3)
    ag_i(2)
    ag_i(3)

    for n in range(2):
        wait(pts_in, g_send.at[n])
        wait(pts.at[:, 0, 0, 0], g_send.at[2 + n])
        wait(pts.at[:, 2 + n, :, c], g_send.at[4 + n])
        wait(pts.at[:, 2 + n, :, c], g_send.at[7 + n])
    wait(pts.at[:, pl.ds(0, 2), :, c], g_send.at[6])
    wait(st_recv, st_ss.at[0])
    wait(z2_recv, z2_ss.at[0])
    wait(ry2, y2_ss.at[0])
    wait(rym, ym_ss.at[0])
    wait(rz, rz_ss.at[0])
    wait(rz, az_ss.at[0])
    wait(outv.at[pl.ds(0, 2)], ay_ss.at[0])
    wait(outv.at[0], ay_ss.at[1])
    wait(cnt_y, c_ss.at[0])
    wait(cnt_z, c_ss.at[1])
    for n in range(4):
        writeback(n).wait()


def on_device(points, centroids):
    dma = pltpu.SemaphoreType.DMA
    out, counts = pl.pallas_call(
        kernel,
        out_shape=(
            jax.ShapeDtypeStruct((4, 4, 4, 16, D), BF16),
            jax.ShapeDtypeStruct((8, 128), F32),
        ),
        in_specs=[pl.BlockSpec(memory_space=pl.ANY)] * 2,
        out_specs=(
            pl.BlockSpec(memory_space=pl.ANY),
            pl.BlockSpec(memory_space=pltpu.VMEM),
        ),
        scratch_shapes=[
            pltpu.VMEM((NS, 4, 4, 2, R, D), BF16),
            pltpu.VMEM((1024, D), BF16),
            pltpu.VMEM((NS, 4, 1024, G), F32),
            pltpu.VMEM((NS, 4, 8, 128), F32),
            pltpu.VMEM((NS, 4, 8, 128), F32),
            pltpu.VMEM((NS, 4, 8, 128), F32),
            pltpu.VMEM((NS, 2, 8, 128), F32),
            pltpu.VMEM((NS, 7, 2, 8, 128), F32),
            pltpu.VMEM((NS, 2, 8, 128), F32),
            pltpu.VMEM((NS, 2, 2, 8, 128), F32),
            pltpu.VMEM((4, 4, 64, D), F32),
            pltpu.VMEM((1024, 128), F32),
            pltpu.VMEM((4, 4, 64, D), BF16),
            pltpu.VMEM((4, 2, 64, D // 2), BF16),
            pltpu.VMEM((4, 2, 64, D), BF16),
            pltpu.VMEM((4, 4, 16, D), F32),
            pltpu.VMEM((4, 4, 16, D), BF16),
            pltpu.VMEM((4, 3, 16, D), BF16),
            pltpu.VMEM((4, 4, 4, 16, D), BF16),
            pltpu.VMEM((2, 8, 128), F32),
            pltpu.VMEM((3, 8, 128), F32),
            pltpu.VMEM((3, 8, 128), F32),
            dma((9,)), dma((NS, 9)), dma((NS,)), dma((1,)), dma((NS,)), dma((1,)), dma((NS,)),
            dma((1,)), dma((4, 2)), dma((1,)), dma((4,)), dma((1,)), dma((4,)),
            dma((1,)), dma((4,)), dma((2,)), dma((4, 4)), dma((2,)), dma((2,)), dma((5,)),
        ],
        compiler_params=pltpu.CompilerParams(
            collective_id=0, has_side_effects=True, vmem_limit_bytes=56 << 20
        ),
        cost_estimate=pl.CostEstimate(
            flops=4 * 4096 * 1024 * D, bytes_accessed=4 << 20, transcendentals=4096 * 1024
        ),
    )(points.reshape(2, 128, D), centroids)
    return out.reshape(1024, D), counts.reshape(1024)


def solution(mesh):
    placed = (P(("wide", "narrow"), None), P("narrow", None))
    return jax.shard_map(
        on_device,
        mesh=mesh,
        in_specs=placed,
        out_specs=(P("narrow", None), P("narrow")),
        check_vma=False,
    )
```

```python
import functools

import jax
import jax.numpy as jnp
from jax import lax
from jax.experimental import pallas as pl
from jax.experimental.pallas import tpu as pltpu
from jax.sharding import PartitionSpec as P

MESH = pl.DeviceIdType.MESH
F32 = jnp.float32
BF16 = jnp.bfloat16
D = 768
NP = 4
R = 128 // NP
KB = 256
RATE = 60.0 * 1.4426950408889634


def kernel(
    pts_in, cen_in, out_ref, cnt_out,
    pts, cen, e, m_tile, t_tile, s_tile, st_one, st_pair, st_chip, st_up, st_down, st_x, st_z,
    acc, cacc, yb, ry2, rym, zt, zb, rz, outv, cnt, cnt_y, cnt_z,
    x_ss, x_rs, f_ss, f_rs, z_ss, z_rs, s_ss, s_rs, sp_ss, sp_rs, sx_ss, sx_rs, sz_ss, sz_rs, far,
    y2_ss, y2_rs, ym_ss, ym_rs, rz_ss, rz_rs, az_ss, az_rs, ay_ss, ay_rs, c_ss, c_rs, io_sem,
):
    wide, narrow = lax.axis_index("wide"), lax.axis_index("narrow")
    h, y = wide // 4, wide % 4
    zl, x, c = narrow // 8, (narrow // 2) % 4, narrow % 2
    z = 2 * h + zl
    xm, xp, x2 = (x + 3) % 4, (x + 1) % 4, (x + 2) % 4
    ym, yp, y2 = (y + 3) % 4, (y + 1) % 4, (y + 2) % 4

    def at(dx=0, dy=0, dz=0, dc=0):
        zz = (z + dz + 8) % 8
        return (
            (zz // 2) * 4 + (y + dy + 4) % 4,
            (zz % 2) * 8 + ((x + dx + 4) % 4) * 2 + (c + dc) % 2,
        )

    def send(src, dst, ss, rs, device):
        return pltpu.make_async_remote_copy(
            src_ref=src, dst_ref=dst, send_sem=ss, recv_sem=rs, device_id=device, device_id_type=MESH
        )

    def wait(ref, sem):
        send(ref, ref, sem, sem, at(dc=1)).wait_recv()

    cen_copy = pltpu.make_async_copy(cen_in, cen, io_sem.at[0])
    local = pltpu.make_async_copy(pts_in, pts.at[x, pl.ds(0, 2), c], io_sem.at[1])
    cen_copy.start()
    local.start()

    partners = [at(dc=1), at(dx=1), at(dx=-1), at(dy=1), at(dy=-1), at(dz=1), at(dz=-1)]
    barrier = pltpu.get_barrier_semaphore()
    for device in partners:
        pl.semaphore_signal(barrier, inc=1, device_id=device, device_id_type=MESH)
    acc[...] = jnp.zeros_like(acc)
    cacc[...] = jnp.zeros_like(cacc)
    pl.semaphore_wait(barrier, len(partners))

    sources = (x, xm, xp, x2)

    def piece(p):
        return pl.ds(p * R, R)

    def xcopy(p, way):
        return send(
            pts_in.at[:, piece(p)], pts.at[x, pl.ds(0, 2), c, piece(p)],
            x_ss.at[0], x_rs.at[p, way], at(dx=1 - 2 * way),
        )

    def fcopy(p, way):
        block = pts.at[(xm, xp)[way], way, c, piece(p)]
        return send(block, block, f_ss.at[0], f_rs.at[p, way], at(dx=1 - 2 * way))

    def zpoints(p, way, k):
        o = sources[k]
        src = pts_in.at[way, piece(p)] if k == 0 else pts.at[o, way, c, piece(p)]
        return send(src, pts.at[o, 2 + way, c, piece(p)], z_ss.at[0], z_rs.at[k], at(dz=1 - 2 * way))

    def sib(k, p=None):
        o, g = sources[k % 4], 2 * (k // 4)
        rows = pl.ds(0, 128) if p is None else piece(p)
        dst = pts.at[o, pl.ds(g, 2), c, rows]
        return send(pts_in if k == 0 else dst, dst, s_ss.at[0], s_rs.at[k], at(dc=1))

    def sib_arrived(k):
        wait(pts.at[0, pl.ds(0, 2), 0], s_rs.at[k])

    def ev0():
        for p in range(NP):
            for way in range(2):
                xcopy(p, way).start()
                zpoints(p, way, 0).start()
        sib(0).start()

    def ev1(p):
        for way in range(2):
            xcopy(p, way).wait_recv()
        for way in range(2):
            fcopy(p, way).start()
            for k in (1, 2):
                zpoints(p, way, k).start()
        for k in (1, 2):
            sib(k, p).start()

    def ev2(p):
        for way in range(2):
            fcopy(p, way).wait_recv()
            zpoints(p, way, 3).start()
        sib(3, p).start()

    def ev3(k):
        wait(pts.at[0, pl.ds(2, 2), c], z_rs.at[k])
        sib(4 + k).start()

    def mm1(i, g):
        p = pts[i, g].reshape(2 * 128, D)
        for k in range(4):
            l = lax.dot_general(
                cen[k * KB : (k + 1) * KB, :], p, (((1,), (1,)), ((), ())), preferred_element_type=F32
            )
            m = jnp.max(l, axis=0, keepdims=True)
            v = jnp.exp2((l - m) * RATE)
            e[i, g, k * KB : (k + 1) * KB, :] = v
            t = jnp.sum(v, axis=0, keepdims=True)
            for j in range(2):
                m_tile[i, k, pl.ds(2 * ((g + (g + 1) // 2) % 4) + j, 1), :] = m[:, j * 128 : (j + 1) * 128]
                t_tile[i, k, pl.ds(2 * ((g + (g + 1) // 2) % 4) + j, 1), :] = t[:, j * 128 : (j + 1) * 128]

    def merge(parts):
        m = functools.reduce(jnp.maximum, [a for a, _ in parts])
        return m, sum(t * jnp.exp2((a - m) * RATE) for a, t in parts)

    def pair_copy(i):
        return send(st_one.at[i], st_pair.at[i], sp_ss.at[0], sp_rs.at[i], at(dc=1))

    def st_a(i):
        m, t = merge([(m_tile[i, k], t_tile[i, k]) for k in range(4)])
        st_one[i, 0] = m
        st_one[i, 1] = t
        pair_copy(i).start()

    def st_b(i):
        pair_copy(i).wait_recv()
        m, t = merge([(st_one[i, 0], st_one[i, 1]), (st_pair[i, 0], st_pair[i, 1])])
        st_chip[i, 0] = m
        st_chip[i, 1] = t
        st_up[i] = jnp.concatenate([m[2:4], m[0:2], t[2:4], t[0:2]], axis=0)
        st_down[i] = jnp.concatenate([m[6:8], m[4:6], t[6:8], t[4:6]], axis=0)
        for d in (2, 1, 3):
            send(st_chip.at[i], st_x.at[i, d - 1], sx_ss.at[0], sx_rs.at[i], at(dx=d)).start()

    def st_c(i):
        for d in (2, 1, 3, 0):
            send(st_up.at[i], st_z.at[i, 0, d], sz_ss.at[0], sz_rs.at[i], at(dx=d, dz=1)).start()
            send(st_down.at[i], st_z.at[i, 1, d], sz_ss.at[0], sz_rs.at[i], at(dx=d, dz=-1)).start()

    def st_d(i, carry):
        wait(st_x.at[i], sx_rs.at[i])
        wait(st_z.at[i], sz_rs.at[i])
        mine = merge([(st_chip[i, 0], st_chip[i, 1])] + [(st_x[i, d, 0], st_x[i, d, 1]) for d in range(3)])
        far_z = [[(st_z[i, w, d][:4], st_z[i, w, d][4:]) for d in range(4)] for w in (1, 0)]
        above, below = merge(far_z[0]), merge(far_z[1])
        other = [jnp.concatenate([a, b], axis=0) for a, b in zip(above, below)]
        m, t = merge([mine, tuple(other)])
        inv = 1.0 / t
        for k in range(4):
            s_tile[i, k] = jnp.exp2((m_tile[i, k] - m) * RATE) * inv
        return carry

    ev0()
    cen_copy.wait()
    local.wait()

    def step(t, carry):
        def before(n, *acts):
            @pl.when(t == n)
            def _():
                for act in acts:
                    act()

        def do(f, *a):
            return functools.partial(f, *a)

        before(0, do(sib_arrived, 0))
        before(1, do(ev1, 0))
        before(2, do(ev1, 1), do(ev3, 0), do(ev1, 2), do(sib_arrived, 4))
        before(4, do(st_a, x), do(ev1, 3), do(ev2, 0), do(sib_arrived, 1))
        before(5, do(ev2, 1), do(st_b, x))
        before(6, do(ev2, 2), do(sib_arrived, 2))
        before(7, do(ev2, 3), do(ev3, 1))
        before(8, do(sib_arrived, 5))
        before(9, do(ev3, 2))
        before(10, do(st_a, xm), do(sib_arrived, 6))
        before(12, do(st_a, xp), do(st_b, xm), do(sib_arrived, 3))
        before(13, do(st_b, xp))
        before(14, do(ev3, 3), do(st_c, x), do(st_c, xm), do(st_c, xp), do(sib_arrived, 7))
        j = t // 4
        mid = (j % 3 + 1) // 2
        off = mid * (3 - 2 * ((t % 4) // 2)) + (1 - mid) * (2 * (j // 3))
        g = mid * ((j - 1) * 2 + t % 2) + (1 - mid) * (t % 4)
        mm1((x + off) % 4, g)
        return carry

    lax.fori_loop(0, 16, step, 0)
    st_a(x2)
    st_b(x2)
    st_c(x2)
    lax.fori_loop(0, 4, st_d, 0)
    for d in (2, -2):
        pl.semaphore_signal(far, inc=1, device_id=at(dz=d), device_id_type=MESH)

    def mm2(n, lo, hi):
        def part(i, carry):
            cs = jnp.zeros((KB, 128), F32)
            resp = []
            for g in range(4):
                for j in range(2):
                    v = e[i, g, n * KB : (n + 1) * KB, j * 128 : (j + 1) * 128]
                    v = v * s_tile[i, n, pl.ds(2 * ((g + (g + 1) // 2) % 4) + j, 1), :]
                    cs = cs + v
                    resp.append(v.astype(BF16))
            cacc[n * KB : (n + 1) * KB, :] += cs
            acc[n] += jnp.dot(
                jnp.concatenate(resp, axis=1), pts[i].reshape(1024, D), preferred_element_type=F32
            ).reshape(4, 64, D)
            return carry

        lax.fori_loop(lo, hi, part, 0)

    def cols(side):
        return pl.ds(side * (D // 2), D // 2)

    def ycopy(n, kind, side):
        to, near = at(dy=1 - 2 * side), (yp, ym)[side]
        if kind == 0:
            return send(yb.at[n, y2, :, cols(side)], ry2.at[n, side], y2_ss.at[0], y2_rs.at[n, side], to)
        part = cols(1 - side if kind == 1 else side)
        return send(yb.at[n, near, :, part], rym.at[n, side, :, part], ym_ss.at[0], ym_rs.at[n], to)

    def rs_a(n):
        yb[n] = acc[n].astype(BF16)
        for kind in range(2):
            for side in range(2):
                ycopy(n, kind, side).start()

    def rs_b(n):
        for side, near in ((0, yp), (1, ym)):
            ycopy(n, 0, side).wait_recv()
            part = cols(side)
            yb[n, near, :, part] = (acc[n, near, :, part] + ry2[n, side].astype(F32)).astype(BF16)
            ycopy(n, 2, side).start()

    def zcopy(n, d):
        return send(zb.at[n, (h + d) % 4], rz.at[n, d - 1], rz_ss.at[0], rz_rs.at[n], at(dz=2 * d))

    def rs_c(n):
        wait(rym.at[n], ym_rs.at[n])
        total = acc[n, y] + rym[n, 0].astype(F32) + rym[n, 1].astype(F32)
        zt[n] = total.reshape(4, 16, D)
        zb[n] = total.astype(BF16).reshape(4, 16, D)
        if n == 0:
            pl.semaphore_wait(far, 2)
        for d in (2, 1, 3):
            zcopy(n, d).start()

    def azcopy(n, d):
        return send(outv.at[n, y, h], outv.at[n, y, h], az_ss.at[0], az_rs.at[n], at(dz=2 * d))

    def aycopy(n, q):
        side = q % 2
        to, ss, rs = at(dy=1 - 2 * side), ay_ss.at[q // 2], ay_rs.at[n, q]
        block = outv.at[n, y] if q < 2 else outv.at[n, (ym, yp)[side], :, :, cols(side)]
        return send(block, block, ss, rs, to)

    def writeback(n):
        return pltpu.make_async_copy(outv.at[n], out_ref.at[n], io_sem.at[2 + n])

    def ag_f(n):
        wait(rz.at[n], rz_rs.at[n])
        total = zt[n, h]
        for d in range(3):
            total = total + rz[n, d].astype(F32)
        scale = lax.rsqrt(jnp.sum(total * total, axis=1, keepdims=True) + 1e-06)
        outv[n, y, h] = (total * scale).astype(BF16)
        for d in (2, 1, 3):
            azcopy(n, d).start()

    def ag_g(n):
        wait(rz.at[n], az_rs.at[n])
        for q in range(2):
            aycopy(n, q).start()

    def ag_h(n):
        for q in range(2):
            aycopy(n, q).wait_recv()
            aycopy(n, 2 + q).start()

    def ag_i(n):
        for q in range(2, 4):
            aycopy(n, q).wait_recv()
        writeback(n).start()

    def ccopy(n):
        d = n % 3 + 1
        if n < 3:
            return send(cnt.at[0], cnt_y.at[d - 1], c_ss.at[0], c_rs.at[0], at(dy=d))
        return send(cnt.at[1], cnt_z.at[d - 1], c_ss.at[1], c_rs.at[1], at(dz=2 * d))

    def cnt_a():
        rest, lanes = cacc[...], jnp.zeros((8, 1024), F32)
        ones = jnp.ones((8, 128), BF16)
        for _ in range(3):
            term = rest.astype(BF16)
            lanes += lax.dot_general(ones, term, (((1,), (1,)), ((), ())), preferred_element_type=F32)
            rest = rest - term.astype(F32)
        row = lax.broadcasted_iota(jnp.int32, (8, 128), 0)
        dense = jnp.zeros((8, 128), F32)
        for r in range(8):
            dense = jnp.where(row == r, lanes[:, r * 128 : (r + 1) * 128], dense)
        cnt[0] = dense
        for n in range(3):
            ccopy(n).start()

    def cnt_b():
        wait(cnt_y, c_rs.at[0])
        cnt[1] = cnt[0] + cnt_y[0] + cnt_y[1] + cnt_y[2]
        for n in range(3, 6):
            ccopy(n).start()

    def cnt_c():
        wait(cnt_z, c_rs.at[1])
        cnt_out[...] = cnt[1] + cnt_z[0] + cnt_z[1] + cnt_z[2]

    mm2(0, 0, 4)
    rs_a(0)
    mm2(1, 0, 4)
    rs_a(1)
    rs_b(0)
    mm2(2, 0, 4)
    rs_a(2)
    rs_b(1)
    rs_c(0)
    mm2(3, 0, 4)
    rs_a(3)
    rs_b(2)
    rs_c(1)
    ag_f(0)
    rs_b(3)
    rs_c(2)
    ag_f(1)
    ag_g(0)
    rs_c(3)
    cnt_a()
    ag_f(2)
    ag_g(1)
    ag_h(0)
    ag_f(3)
    ag_g(2)
    cnt_b()
    ag_i(0)
    ag_h(1)
    ag_g(3)
    ag_i(1)
    ag_h(2)
    cnt_c()
    ag_i(2)
    ag_h(3)
    ag_i(3)

    wait(pts.at[0, pl.ds(0, 2)], x_ss.at[0])
    wait(pts.at[0, 0], f_ss.at[0])
    wait(pts.at[0], z_ss.at[0])
    wait(pts.at[pl.ds(0, 2)], s_ss.at[0])
    wait(st_pair, sp_ss.at[0])
    wait(st_x, sx_ss.at[0])
    wait(st_z, sz_ss.at[0])
    wait(ry2, y2_ss.at[0])
    wait(rym, ym_ss.at[0])
    wait(rz, rz_ss.at[0])
    wait(rz, az_ss.at[0])
    wait(outv.at[pl.ds(0, 2)], ay_ss.at[0])
    wait(outv.at[0], ay_ss.at[1])
    wait(cnt_y, c_ss.at[0])
    wait(cnt_z, c_ss.at[1])
    for n in range(4):
        writeback(n).wait()


def on_device(points, centroids):
    dma = pltpu.SemaphoreType.DMA
    out, counts = pl.pallas_call(
        kernel,
        out_shape=(
            jax.ShapeDtypeStruct((4, 4, 4, 16, D), BF16),
            jax.ShapeDtypeStruct((8, 128), F32),
        ),
        in_specs=[pl.BlockSpec(memory_space=pl.ANY)] * 2,
        out_specs=(
            pl.BlockSpec(memory_space=pl.ANY),
            pl.BlockSpec(memory_space=pltpu.VMEM),
        ),
        scratch_shapes=[
            pltpu.VMEM((4, 4, 2, 128, D), BF16),
            pltpu.VMEM((1024, D), BF16),
            pltpu.VMEM((4, 4, 1024, 256), F32),
            pltpu.VMEM((4, 4, 8, 128), F32),
            pltpu.VMEM((4, 4, 8, 128), F32),
            pltpu.VMEM((4, 4, 8, 128), F32),
            pltpu.VMEM((4, 2, 8, 128), F32),
            pltpu.VMEM((4, 2, 8, 128), F32),
            pltpu.VMEM((4, 2, 8, 128), F32),
            pltpu.VMEM((4, 8, 128), F32),
            pltpu.VMEM((4, 8, 128), F32),
            pltpu.VMEM((4, 3, 2, 8, 128), F32),
            pltpu.VMEM((4, 2, 4, 8, 128), F32),
            pltpu.VMEM((4, 4, 64, D), F32),
            pltpu.VMEM((1024, 128), F32),
            pltpu.VMEM((4, 4, 64, D), BF16),
            pltpu.VMEM((4, 2, 64, D // 2), BF16),
            pltpu.VMEM((4, 2, 64, D), BF16),
            pltpu.VMEM((4, 4, 16, D), F32),
            pltpu.VMEM((4, 4, 16, D), BF16),
            pltpu.VMEM((4, 3, 16, D), BF16),
            pltpu.VMEM((4, 4, 4, 16, D), BF16),
            pltpu.VMEM((2, 8, 128), F32),
            pltpu.VMEM((3, 8, 128), F32),
            pltpu.VMEM((3, 8, 128), F32),
            dma((1,)), dma((NP, 2)), dma((1,)), dma((NP, 2)), dma((1,)), dma((4,)), dma((1,)), dma((8,)),
            dma((1,)), dma((4,)), dma((1,)), dma((4,)), dma((1,)), dma((4,)), pltpu.SemaphoreType.REGULAR,
            dma((1,)), dma((4, 2)), dma((1,)), dma((4,)), dma((1,)), dma((4,)),
            dma((1,)), dma((4,)), dma((2,)), dma((4, 4)), dma((2,)), dma((2,)), dma((6,)),
        ],
        compiler_params=pltpu.CompilerParams(
            collective_id=0, has_side_effects=True, vmem_limit_bytes=56 << 20
        ),
        cost_estimate=pl.CostEstimate(
            flops=4 * 4096 * 1024 * D, bytes_accessed=4 << 20, transcendentals=4096 * 1024
        ),
    )(points.reshape(2, 128, D), centroids)
    return out.reshape(1024, D), counts.reshape(1024)


def solution(mesh):
    placed = (P(("wide", "narrow"), None), P("narrow", None))
    return jax.shard_map(
        on_device,
        mesh=mesh,
        in_specs=placed,
        out_specs=(P("narrow", None), P("narrow")),
        check_vma=False,
    )
```

```python
import functools

import jax
import jax.numpy as jnp
from jax import lax
from jax.experimental import pallas as pl
from jax.experimental.pallas import tpu as pltpu
from jax.sharding import PartitionSpec as P

MESH = pl.DeviceIdType.MESH
F32 = jnp.float32
BF16 = jnp.bfloat16
D = 768
NP = 4
R = 128 // NP
KB = 256
RATE = 60.0 * 1.4426950408889634


def kernel(
    pts_in, cen_in, out_ref, cnt_out,
    pts, cen, e, m_tile, t_tile, s_tile, st_one, st_pair, st_chip, st_up, st_down, st_x, st_z,
    acc, cacc, yb, ry2, rym, zt, zb, rz, outv, cnt, cnt_y, cnt_z,
    x_ss, x_rs, f_ss, f_rs, z_ss, z_rs, s_ss, s_rs, sp_ss, sp_rs, sx_ss, sx_rs, sz_ss, sz_rs, far,
    y2_ss, y2_rs, ym_ss, ym_rs, rz_ss, rz_rs, az_ss, az_rs, ay_ss, ay_rs, c_ss, c_rs, io_sem,
):
    wide, narrow = lax.axis_index("wide"), lax.axis_index("narrow")
    h, y = wide // 4, wide % 4
    zl, x, c = narrow // 8, (narrow // 2) % 4, narrow % 2
    z = 2 * h + zl
    xm, xp, x2 = (x + 3) % 4, (x + 1) % 4, (x + 2) % 4
    ym, yp, y2 = (y + 3) % 4, (y + 1) % 4, (y + 2) % 4

    def at(dx=0, dy=0, dz=0, dc=0):
        zz = (z + dz + 8) % 8
        return (
            (zz // 2) * 4 + (y + dy + 4) % 4,
            (zz % 2) * 8 + ((x + dx + 4) % 4) * 2 + (c + dc) % 2,
        )

    def send(src, dst, ss, rs, device):
        return pltpu.make_async_remote_copy(
            src_ref=src, dst_ref=dst, send_sem=ss, recv_sem=rs, device_id=device, device_id_type=MESH
        )

    def wait(ref, sem):
        send(ref, ref, sem, sem, at(dc=1)).wait_recv()

    cen_copy = pltpu.make_async_copy(cen_in, cen, io_sem.at[0])
    local = pltpu.make_async_copy(pts_in, pts.at[x, pl.ds(0, 2), c], io_sem.at[1])
    cen_copy.start()
    local.start()

    partners = [at(dc=1), at(dx=1), at(dx=-1), at(dy=1), at(dy=-1), at(dz=1), at(dz=-1)]
    barrier = pltpu.get_barrier_semaphore()
    for device in partners:
        pl.semaphore_signal(barrier, inc=1, device_id=device, device_id_type=MESH)
    acc[...] = jnp.zeros_like(acc)
    cacc[...] = jnp.zeros_like(cacc)
    pl.semaphore_wait(barrier, len(partners))

    sources = (x, xm, xp, x2)

    def piece(p):
        return pl.ds(p * R, R)

    def xcopy(p, way):
        return send(
            pts_in.at[:, piece(p)], pts.at[x, pl.ds(0, 2), c, piece(p)],
            x_ss.at[0], x_rs.at[p, way], at(dx=1 - 2 * way),
        )

    def fcopy(p, way):
        block = pts.at[(xm, xp)[way], way, c, piece(p)]
        return send(block, block, f_ss.at[0], f_rs.at[p, way], at(dx=1 - 2 * way))

    def zpoints(p, way, k):
        o = sources[k]
        src = pts_in.at[way, piece(p)] if k == 0 else pts.at[o, way, c, piece(p)]
        return send(src, pts.at[o, 2 + way, c, piece(p)], z_ss.at[0], z_rs.at[k], at(dz=1 - 2 * way))

    def sib(k, p=None):
        o, g = sources[k % 4], 2 * (k // 4)
        rows = pl.ds(0, 128) if p is None else piece(p)
        dst = pts.at[o, pl.ds(g, 2), c, rows]
        return send(pts_in if k == 0 else dst, dst, s_ss.at[0], s_rs.at[k], at(dc=1))

    def sib_arrived(k):
        wait(pts.at[0, pl.ds(0, 2), 0], s_rs.at[k])

    def ev0():
        for p in range(NP):
            for way in range(2):
                xcopy(p, way).start()
                zpoints(p, way, 0).start()
        sib(0).start()

    def ev1(p):
        for way in range(2):
            xcopy(p, way).wait_recv()
        for way in range(2):
            fcopy(p, way).start()
            for k in (1, 2):
                zpoints(p, way, k).start()
        for k in (1, 2):
            sib(k, p).start()

    def ev2(p):
        for way in range(2):
            fcopy(p, way).wait_recv()
            zpoints(p, way, 3).start()
        sib(3, p).start()

    def ev3(k):
        wait(pts.at[0, pl.ds(2, 2), c], z_rs.at[k])
        sib(4 + k).start()

    def mm1(i, w):
        p = pts[i, pl.ds(2 * w, 2)].reshape(512, D)
        for k in range(4):
            l = lax.dot_general(
                cen[k * KB : (k + 1) * KB, :], p, (((1,), (1,)), ((), ())), preferred_element_type=F32
            )
            m = jnp.max(l, axis=0, keepdims=True)
            v = jnp.exp2((l - m) * RATE)
            t = jnp.sum(v, axis=0, keepdims=True)
            for q in range(2):
                g = 2 * w + q
                e[i, g, k * KB : (k + 1) * KB, :] = v[:, q * 256 : (q + 1) * 256]
                for j in range(2):
                    row = pl.ds(2 * ((g + (g + 1) // 2) % 4) + j, 1)
                    lanes = slice(q * 256 + j * 128, q * 256 + (j + 1) * 128)
                    m_tile[i, k, row, :] = m[:, lanes]
                    t_tile[i, k, row, :] = t[:, lanes]

    def merge(parts):
        m = functools.reduce(jnp.maximum, [a for a, _ in parts])
        return m, sum(t * jnp.exp2((a - m) * RATE) for a, t in parts)

    def pair_copy(i):
        return send(st_one.at[i], st_pair.at[i], sp_ss.at[0], sp_rs.at[i], at(dc=1))

    def st_a(i):
        m, t = merge([(m_tile[i, k], t_tile[i, k]) for k in range(4)])
        st_one[i, 0] = m
        st_one[i, 1] = t
        pair_copy(i).start()

    def st_b(i):
        pair_copy(i).wait_recv()
        m, t = merge([(st_one[i, 0], st_one[i, 1]), (st_pair[i, 0], st_pair[i, 1])])
        st_chip[i, 0] = m
        st_chip[i, 1] = t
        st_up[i] = jnp.concatenate([m[2:4], m[0:2], t[2:4], t[0:2]], axis=0)
        st_down[i] = jnp.concatenate([m[6:8], m[4:6], t[6:8], t[4:6]], axis=0)
        for d in (2, 1, 3):
            send(st_chip.at[i], st_x.at[i, d - 1], sx_ss.at[0], sx_rs.at[i], at(dx=d)).start()

    def st_c(i):
        for d in (2, 1, 3, 0):
            send(st_up.at[i], st_z.at[i, 0, d], sz_ss.at[0], sz_rs.at[i], at(dx=d, dz=1)).start()
            send(st_down.at[i], st_z.at[i, 1, d], sz_ss.at[0], sz_rs.at[i], at(dx=d, dz=-1)).start()

    def st_d(i, carry):
        wait(st_x.at[i], sx_rs.at[i])
        wait(st_z.at[i], sz_rs.at[i])
        mine = merge([(st_chip[i, 0], st_chip[i, 1])] + [(st_x[i, d, 0], st_x[i, d, 1]) for d in range(3)])
        far_z = [[(st_z[i, w, d][:4], st_z[i, w, d][4:]) for d in range(4)] for w in (1, 0)]
        above, below = merge(far_z[0]), merge(far_z[1])
        other = [jnp.concatenate([a, b], axis=0) for a, b in zip(above, below)]
        m, t = merge([mine, tuple(other)])
        inv = 1.0 / t
        for k in range(4):
            s_tile[i, k] = jnp.exp2((m_tile[i, k] - m) * RATE) * inv
        return carry

    ev0()
    cen_copy.wait()
    local.wait()

    def step(t, carry):
        def before(n, *acts):
            @pl.when(t == n)
            def _():
                for act in acts:
                    act()

        def do(f, *a):
            return functools.partial(f, *a)

        before(0, do(sib_arrived, 0))
        before(1, do(ev1, 0), do(ev1, 1), do(ev3, 0), do(ev1, 2), do(sib_arrived, 4))
        before(2, do(st_a, x), do(ev1, 3), do(ev2, 0), do(sib_arrived, 1))
        before(3, do(ev2, 1), do(sib_arrived, 2), do(st_b, x))
        before(4, do(ev2, 2), do(ev2, 3), do(ev3, 1), do(ev3, 2), do(sib_arrived, 5))
        before(5, do(st_a, xm), do(sib_arrived, 6))
        before(6, do(st_a, xp), do(st_b, xm), do(ev3, 3), do(sib_arrived, 3))
        before(7, do(st_b, xp), do(st_c, x), do(st_c, xm), do(st_c, xp), do(sib_arrived, 7))
        j = t // 2
        mid = (j % 3 + 1) // 2
        off = mid * (3 - 2 * (t % 2)) + (1 - mid) * (2 * (j // 3))
        mm1((x + off) % 4, mid * (j - 1) + (1 - mid) * (t % 2))
        return carry

    lax.fori_loop(0, 8, step, 0)
    st_a(x2)
    st_b(x2)
    st_c(x2)
    lax.fori_loop(0, 4, st_d, 0)
    for d in (2, -2):
        pl.semaphore_signal(far, inc=1, device_id=at(dz=d), device_id_type=MESH)

    def mm2(n, lo, hi):
        def part(i, carry):
            cs = jnp.zeros((KB, 128), F32)
            resp = []
            for g in range(4):
                for j in range(2):
                    v = e[i, g, n * KB : (n + 1) * KB, j * 128 : (j + 1) * 128]
                    v = v * s_tile[i, n, pl.ds(2 * ((g + (g + 1) // 2) % 4) + j, 1), :]
                    cs = cs + v
                    resp.append(v.astype(BF16))
            cacc[n * KB : (n + 1) * KB, :] += cs
            acc[n] += jnp.dot(
                jnp.concatenate(resp, axis=1), pts[i].reshape(1024, D), preferred_element_type=F32
            ).reshape(4, 64, D)
            return carry

        lax.fori_loop(lo, hi, part, 0)

    def cols(side):
        return pl.ds(side * (D // 2), D // 2)

    def ycopy(n, kind, side):
        to, near = at(dy=1 - 2 * side), (yp, ym)[side]
        if kind == 0:
            return send(yb.at[n, y2, :, cols(side)], ry2.at[n, side], y2_ss.at[0], y2_rs.at[n, side], to)
        part = cols(1 - side if kind == 1 else side)
        return send(yb.at[n, near, :, part], rym.at[n, side, :, part], ym_ss.at[0], ym_rs.at[n], to)

    def rs_a(n):
        yb[n] = acc[n].astype(BF16)
        for kind in range(2):
            for side in range(2):
                ycopy(n, kind, side).start()

    def rs_b(n):
        for side, near in ((0, yp), (1, ym)):
            ycopy(n, 0, side).wait_recv()
            part = cols(side)
            yb[n, near, :, part] = (acc[n, near, :, part] + ry2[n, side].astype(F32)).astype(BF16)
            ycopy(n, 2, side).start()

    def zcopy(n, d):
        return send(zb.at[n, (h + d) % 4], rz.at[n, d - 1], rz_ss.at[0], rz_rs.at[n], at(dz=2 * d))

    def rs_c(n):
        wait(rym.at[n], ym_rs.at[n])
        total = acc[n, y] + rym[n, 0].astype(F32) + rym[n, 1].astype(F32)
        zt[n] = total.reshape(4, 16, D)
        zb[n] = total.astype(BF16).reshape(4, 16, D)
        if n == 0:
            pl.semaphore_wait(far, 2)
        for d in (2, 1, 3):
            zcopy(n, d).start()

    def azcopy(n, d):
        return send(outv.at[n, y, h], outv.at[n, y, h], az_ss.at[0], az_rs.at[n], at(dz=2 * d))

    def aycopy(n, q):
        side = q % 2
        to, ss, rs = at(dy=1 - 2 * side), ay_ss.at[q // 2], ay_rs.at[n, q]
        block = outv.at[n, y] if q < 2 else outv.at[n, (ym, yp)[side], :, :, cols(side)]
        return send(block, block, ss, rs, to)

    def writeback(n):
        return pltpu.make_async_copy(outv.at[n], out_ref.at[n], io_sem.at[2 + n])

    def ag_f(n):
        wait(rz.at[n], rz_rs.at[n])
        total = zt[n, h]
        for d in range(3):
            total = total + rz[n, d].astype(F32)
        scale = lax.rsqrt(jnp.sum(total * total, axis=1, keepdims=True) + 1e-06)
        outv[n, y, h] = (total * scale).astype(BF16)
        for d in (2, 1, 3):
            azcopy(n, d).start()

    def ag_g(n):
        wait(rz.at[n], az_rs.at[n])
        for q in range(2):
            aycopy(n, q).start()

    def ag_h(n):
        for q in range(2):
            aycopy(n, q).wait_recv()
            aycopy(n, 2 + q).start()

    def ag_i(n):
        for q in range(2, 4):
            aycopy(n, q).wait_recv()
        writeback(n).start()

    def ccopy(n):
        d = n % 3 + 1
        if n < 3:
            return send(cnt.at[0], cnt_y.at[d - 1], c_ss.at[0], c_rs.at[0], at(dy=d))
        return send(cnt.at[1], cnt_z.at[d - 1], c_ss.at[1], c_rs.at[1], at(dz=2 * d))

    def cnt_a():
        rest, lanes = cacc[...], jnp.zeros((8, 1024), F32)
        ones = jnp.ones((8, 128), BF16)
        for _ in range(3):
            term = rest.astype(BF16)
            lanes += lax.dot_general(ones, term, (((1,), (1,)), ((), ())), preferred_element_type=F32)
            rest = rest - term.astype(F32)
        row = lax.broadcasted_iota(jnp.int32, (8, 128), 0)
        dense = jnp.zeros((8, 128), F32)
        for r in range(8):
            dense = jnp.where(row == r, lanes[:, r * 128 : (r + 1) * 128], dense)
        cnt[0] = dense
        for n in range(3):
            ccopy(n).start()

    def cnt_b():
        wait(cnt_y, c_rs.at[0])
        cnt[1] = cnt[0] + cnt_y[0] + cnt_y[1] + cnt_y[2]
        for n in range(3, 6):
            ccopy(n).start()

    def cnt_c():
        wait(cnt_z, c_rs.at[1])
        cnt_out[...] = cnt[1] + cnt_z[0] + cnt_z[1] + cnt_z[2]

    mm2(0, 0, 4)
    rs_a(0)
    mm2(1, 0, 4)
    rs_a(1)
    rs_b(0)
    mm2(2, 0, 4)
    rs_a(2)
    rs_b(1)
    rs_c(0)
    mm2(3, 0, 4)
    rs_a(3)
    rs_b(2)
    rs_c(1)
    ag_f(0)
    rs_b(3)
    rs_c(2)
    ag_f(1)
    rs_c(3)
    ag_g(0)
    ag_f(2)
    cnt_a()
    ag_g(1)
    ag_h(0)
    ag_f(3)
    ag_g(2)
    ag_h(1)
    cnt_b()
    ag_g(3)
    ag_h(2)
    ag_h(3)
    cnt_c()
    ag_i(0)
    ag_i(1)
    ag_i(2)
    ag_i(3)

    wait(pts.at[0, pl.ds(0, 2)], x_ss.at[0])
    wait(pts.at[0, 0], f_ss.at[0])
    wait(pts.at[0], z_ss.at[0])
    wait(pts.at[pl.ds(0, 2)], s_ss.at[0])
    wait(st_pair, sp_ss.at[0])
    wait(st_x, sx_ss.at[0])
    wait(st_z, sz_ss.at[0])
    wait(ry2, y2_ss.at[0])
    wait(rym, ym_ss.at[0])
    wait(rz, rz_ss.at[0])
    wait(rz, az_ss.at[0])
    wait(outv.at[pl.ds(0, 2)], ay_ss.at[0])
    wait(outv.at[0], ay_ss.at[1])
    wait(cnt_y, c_ss.at[0])
    wait(cnt_z, c_ss.at[1])
    for n in range(4):
        writeback(n).wait()


def on_device(points, centroids):
    dma = pltpu.SemaphoreType.DMA
    out, counts = pl.pallas_call(
        kernel,
        out_shape=(
            jax.ShapeDtypeStruct((4, 4, 4, 16, D), BF16),
            jax.ShapeDtypeStruct((8, 128), F32),
        ),
        in_specs=[pl.BlockSpec(memory_space=pl.ANY)] * 2,
        out_specs=(
            pl.BlockSpec(memory_space=pl.ANY),
            pl.BlockSpec(memory_space=pltpu.VMEM),
        ),
        scratch_shapes=[
            pltpu.VMEM((4, 4, 2, 128, D), BF16),
            pltpu.VMEM((1024, D), BF16),
            pltpu.VMEM((4, 4, 1024, 256), F32),
            pltpu.VMEM((4, 4, 8, 128), F32),
            pltpu.VMEM((4, 4, 8, 128), F32),
            pltpu.VMEM((4, 4, 8, 128), F32),
            pltpu.VMEM((4, 2, 8, 128), F32),
            pltpu.VMEM((4, 2, 8, 128), F32),
            pltpu.VMEM((4, 2, 8, 128), F32),
            pltpu.VMEM((4, 8, 128), F32),
            pltpu.VMEM((4, 8, 128), F32),
            pltpu.VMEM((4, 3, 2, 8, 128), F32),
            pltpu.VMEM((4, 2, 4, 8, 128), F32),
            pltpu.VMEM((4, 4, 64, D), F32),
            pltpu.VMEM((1024, 128), F32),
            pltpu.VMEM((4, 4, 64, D), BF16),
            pltpu.VMEM((4, 2, 64, D // 2), BF16),
            pltpu.VMEM((4, 2, 64, D), BF16),
            pltpu.VMEM((4, 4, 16, D), F32),
            pltpu.VMEM((4, 4, 16, D), BF16),
            pltpu.VMEM((4, 3, 16, D), BF16),
            pltpu.VMEM((4, 4, 4, 16, D), BF16),
            pltpu.VMEM((2, 8, 128), F32),
            pltpu.VMEM((3, 8, 128), F32),
            pltpu.VMEM((3, 8, 128), F32),
            dma((1,)), dma((NP, 2)), dma((1,)), dma((NP, 2)), dma((1,)), dma((4,)), dma((1,)), dma((8,)),
            dma((1,)), dma((4,)), dma((1,)), dma((4,)), dma((1,)), dma((4,)), pltpu.SemaphoreType.REGULAR,
            dma((1,)), dma((4, 2)), dma((1,)), dma((4,)), dma((1,)), dma((4,)),
            dma((1,)), dma((4,)), dma((2,)), dma((4, 4)), dma((2,)), dma((2,)), dma((6,)),
        ],
        compiler_params=pltpu.CompilerParams(
            collective_id=0, has_side_effects=True, vmem_limit_bytes=56 << 20
        ),
        cost_estimate=pl.CostEstimate(
            flops=4 * 4096 * 1024 * D, bytes_accessed=4 << 20, transcendentals=4096 * 1024
        ),
    )(points.reshape(2, 128, D), centroids)
    return out.reshape(1024, D), counts.reshape(1024)


def solution(mesh):
    placed = (P(("wide", "narrow"), None), P("narrow", None))
    return jax.shard_map(
        on_device,
        mesh=mesh,
        in_specs=placed,
        out_specs=(P("narrow", None), P("narrow")),
        check_vma=False,
    )
```

```python
import functools

import jax
import jax.numpy as jnp
from jax import lax
from jax.experimental import pallas as pl
from jax.experimental.pallas import tpu as pltpu
from jax.sharding import PartitionSpec as P

MESH = pl.DeviceIdType.MESH
F32 = jnp.float32
BF16 = jnp.bfloat16
D = 768
NP = 4
R = 128 // NP
KB = 256
RATE = 60.0 * 1.4426950408889634


def kernel(
    pts_in, cen_in, outv, cnt_out,
    pts, cen, e, m_tile, t_tile, s_tile, st_one, st_pair, st_chip, st_up, st_down, st_x, st_z,
    acc, cacc, yb, ry2, rym, zt, zb, rz, cnt, cnt_y, cnt_z,
    x_ss, x_rs, f_ss, f_rs, z_ss, z_rs, s_ss, s_rs, sp_ss, sp_rs, sx_ss, sx_rs, sz_ss, sz_rs, far,
    y2_ss, y2_rs, ym_ss, ym_rs, rz_ss, rz_rs, az_ss, az_rs, ay_ss, ay_rs, c_ss, c_rs, io_sem,
):
    wide, narrow = lax.axis_index("wide"), lax.axis_index("narrow")
    h, y = wide // 4, wide % 4
    zl, x, c = narrow // 8, (narrow // 2) % 4, narrow % 2
    z = 2 * h + zl
    xm, xp, x2 = (x + 3) % 4, (x + 1) % 4, (x + 2) % 4
    ym, yp, y2 = (y + 3) % 4, (y + 1) % 4, (y + 2) % 4

    def at(dx=0, dy=0, dz=0, dc=0):
        zz = (z + dz + 8) % 8
        return (
            (zz // 2) * 4 + (y + dy + 4) % 4,
            (zz % 2) * 8 + ((x + dx + 4) % 4) * 2 + (c + dc) % 2,
        )

    def send(src, dst, ss, rs, device):
        return pltpu.make_async_remote_copy(
            src_ref=src, dst_ref=dst, send_sem=ss, recv_sem=rs, device_id=device, device_id_type=MESH
        )

    def wait(ref, sem):
        send(ref, ref, sem, sem, at(dc=1)).wait_recv()

    cen_copy = pltpu.make_async_copy(cen_in, cen, io_sem.at[0])
    local = pltpu.make_async_copy(pts_in, pts.at[x, pl.ds(0, 2), c], io_sem.at[1])
    cen_copy.start()
    local.start()

    partners = [at(dc=1), at(dx=1), at(dx=-1), at(dy=1), at(dy=-1), at(dz=1), at(dz=-1)]
    barrier = pltpu.get_barrier_semaphore()
    for device in partners:
        pl.semaphore_signal(barrier, inc=1, device_id=device, device_id_type=MESH)
    acc[...] = jnp.zeros_like(acc)
    cacc[...] = jnp.zeros_like(cacc)
    pl.semaphore_wait(barrier, len(partners))

    sources = (x, xm, xp, x2)

    def piece(p):
        return pl.ds(p * R, R)

    def xcopy(p, way):
        return send(
            pts_in.at[:, piece(p)], pts.at[x, pl.ds(0, 2), c, piece(p)],
            x_ss.at[0], x_rs.at[p, way], at(dx=1 - 2 * way),
        )

    def fcopy(p, way):
        block = pts.at[(xm, xp)[way], way, c, piece(p)]
        return send(block, block, f_ss.at[0], f_rs.at[p, way], at(dx=1 - 2 * way))

    def zpoints(p, way, k):
        o = sources[k]
        src = pts_in.at[way, piece(p)] if k == 0 else pts.at[o, way, c, piece(p)]
        return send(src, pts.at[o, 2 + way, c, piece(p)], z_ss.at[0], z_rs.at[k], at(dz=1 - 2 * way))

    def sib(k, p=None):
        o, g = sources[k % 4], 2 * (k // 4)
        rows = pl.ds(0, 128) if p is None else piece(p)
        dst = pts.at[o, pl.ds(g, 2), c, rows]
        return send(pts_in if k == 0 else dst, dst, s_ss.at[0], s_rs.at[k], at(dc=1))

    def sib_arrived(k):
        wait(pts.at[0, pl.ds(0, 2), 0], s_rs.at[k])

    def ev0():
        for p in range(NP):
            for way in range(2):
                xcopy(p, way).start()
                zpoints(p, way, 0).start()
        sib(0).start()

    def ev1(p):
        for way in range(2):
            xcopy(p, way).wait_recv()
        for way in range(2):
            fcopy(p, way).start()
            for k in (1, 2):
                zpoints(p, way, k).start()
        for k in (1, 2):
            sib(k, p).start()

    def ev2(p):
        for way in range(2):
            fcopy(p, way).wait_recv()
            zpoints(p, way, 3).start()
        sib(3, p).start()

    def ev3(k):
        wait(pts.at[0, pl.ds(2, 2), c], z_rs.at[k])
        sib(4 + k).start()

    def mm1(i, w):
        p = pts[i, pl.ds(2 * w, 2)].reshape(512, D)
        for k in range(4):
            l = lax.dot_general(
                cen[k * KB : (k + 1) * KB, :], p, (((1,), (1,)), ((), ())), preferred_element_type=F32
            )
            m = jnp.max(l, axis=0, keepdims=True)
            v = jnp.exp2((l - m) * RATE)
            t = jnp.sum(v, axis=0, keepdims=True)
            for q in range(2):
                g = 2 * w + q
                e[i, g, k * KB : (k + 1) * KB, :] = v[:, q * 256 : (q + 1) * 256]
                for j in range(2):
                    row = pl.ds(2 * ((g + (g + 1) // 2) % 4) + j, 1)
                    lanes = slice(q * 256 + j * 128, q * 256 + (j + 1) * 128)
                    m_tile[i, k, row, :] = m[:, lanes]
                    t_tile[i, k, row, :] = t[:, lanes]

    def merge(parts):
        m = functools.reduce(jnp.maximum, [a for a, _ in parts])
        return m, sum(t * jnp.exp2((a - m) * RATE) for a, t in parts)

    def pair_copy(i):
        return send(st_one.at[i], st_pair.at[i], sp_ss.at[0], sp_rs.at[i], at(dc=1))

    def st_a(i):
        m, t = merge([(m_tile[i, k], t_tile[i, k]) for k in range(4)])
        st_one[i, 0] = m
        st_one[i, 1] = t
        pair_copy(i).start()

    def st_b(i):
        pair_copy(i).wait_recv()
        m, t = merge([(st_one[i, 0], st_one[i, 1]), (st_pair[i, 0], st_pair[i, 1])])
        st_chip[i, 0] = m
        st_chip[i, 1] = t
        st_up[i] = jnp.concatenate([m[2:4], m[0:2], t[2:4], t[0:2]], axis=0)
        st_down[i] = jnp.concatenate([m[6:8], m[4:6], t[6:8], t[4:6]], axis=0)
        for d in (2, 1, 3):
            send(st_chip.at[i], st_x.at[i, d - 1], sx_ss.at[0], sx_rs.at[i], at(dx=d)).start()

    def st_c(i):
        for d in (2, 1, 3, 0):
            send(st_up.at[i], st_z.at[i, 0, d], sz_ss.at[0], sz_rs.at[i], at(dx=d, dz=1)).start()
            send(st_down.at[i], st_z.at[i, 1, d], sz_ss.at[0], sz_rs.at[i], at(dx=d, dz=-1)).start()

    def st_d(i, carry):
        wait(st_x.at[i], sx_rs.at[i])
        wait(st_z.at[i], sz_rs.at[i])
        mine = merge([(st_chip[i, 0], st_chip[i, 1])] + [(st_x[i, d, 0], st_x[i, d, 1]) for d in range(3)])
        far_z = [[(st_z[i, w, d][:4], st_z[i, w, d][4:]) for d in range(4)] for w in (1, 0)]
        above, below = merge(far_z[0]), merge(far_z[1])
        other = [jnp.concatenate([a, b], axis=0) for a, b in zip(above, below)]
        m, t = merge([mine, tuple(other)])
        inv = 1.0 / t
        for k in range(4):
            s_tile[i, k] = jnp.exp2((m_tile[i, k] - m) * RATE) * inv
        return carry

    ev0()
    cen_copy.wait()
    local.wait()

    def step(t, carry):
        def before(n, *acts):
            @pl.when(t == n)
            def _():
                for act in acts:
                    act()

        def do(f, *a):
            return functools.partial(f, *a)

        before(0, do(sib_arrived, 0))
        before(1, do(ev1, 0), do(ev1, 1), do(ev3, 0), do(ev1, 2), do(sib_arrived, 4))
        before(2, do(st_a, x), do(ev1, 3), do(ev2, 0), do(sib_arrived, 1))
        before(3, do(ev2, 1), do(sib_arrived, 2), do(st_b, x))
        before(4, do(ev2, 2), do(ev2, 3), do(ev3, 1), do(ev3, 2), do(sib_arrived, 5))
        before(5, do(st_a, xm), do(sib_arrived, 6))
        before(6, do(st_a, xp), do(st_b, xm), do(ev3, 3), do(sib_arrived, 3))
        before(7, do(st_b, xp), do(st_c, x), do(st_c, xm), do(st_c, xp), do(sib_arrived, 7))
        j = t // 2
        mid = (j % 3 + 1) // 2
        off = mid * (3 - 2 * (t % 2)) + (1 - mid) * (2 * (j // 3))
        mm1((x + off) % 4, mid * (j - 1) + (1 - mid) * (t % 2))
        return carry

    lax.fori_loop(0, 8, step, 0)
    st_a(x2)
    st_b(x2)
    st_c(x2)
    lax.fori_loop(0, 4, st_d, 0)
    for d in (2, -2):
        pl.semaphore_signal(far, inc=1, device_id=at(dz=d), device_id_type=MESH)

    def mm2(n, lo, hi):
        def part(i, carry):
            cs = jnp.zeros((KB, 128), F32)
            resp = []
            for g in range(4):
                for j in range(2):
                    v = e[i, g, n * KB : (n + 1) * KB, j * 128 : (j + 1) * 128]
                    v = v * s_tile[i, n, pl.ds(2 * ((g + (g + 1) // 2) % 4) + j, 1), :]
                    cs = cs + v
                    resp.append(v.astype(BF16))
            cacc[n * KB : (n + 1) * KB, :] += cs
            acc[n] += jnp.dot(
                jnp.concatenate(resp, axis=1), pts[i].reshape(1024, D), preferred_element_type=F32
            ).reshape(4, 64, D)
            return carry

        lax.fori_loop(lo, hi, part, 0)

    def cols(side):
        return pl.ds(side * (D // 2), D // 2)

    def ycopy(n, kind, side):
        to, near = at(dy=1 - 2 * side), (yp, ym)[side]
        if kind == 0:
            return send(yb.at[n, y2, :, cols(side)], ry2.at[n, side], y2_ss.at[0], y2_rs.at[n, side], to)
        part = cols(1 - side if kind == 1 else side)
        return send(yb.at[n, near, :, part], rym.at[n, side, :, part], ym_ss.at[0], ym_rs.at[n], to)

    def rs_a(n):
        yb[n] = acc[n].astype(BF16)
        for kind in range(2):
            for side in range(2):
                ycopy(n, kind, side).start()

    def rs_b(n):
        for side, near in ((0, yp), (1, ym)):
            ycopy(n, 0, side).wait_recv()
            part = cols(side)
            yb[n, near, :, part] = (acc[n, near, :, part] + ry2[n, side].astype(F32)).astype(BF16)
            ycopy(n, 2, side).start()

    def zcopy(n, d):
        return send(zb.at[n, (h + d) % 4], rz.at[n, d - 1], rz_ss.at[0], rz_rs.at[n], at(dz=2 * d))

    def rs_c(n):
        wait(rym.at[n], ym_rs.at[n])
        total = acc[n, y] + rym[n, 0].astype(F32) + rym[n, 1].astype(F32)
        zt[n] = total.reshape(4, 16, D)
        zb[n] = total.astype(BF16).reshape(4, 16, D)
        if n == 0:
            pl.semaphore_wait(far, 2)
        for d in (2, 1, 3):
            zcopy(n, d).start()

    def azcopy(n, d):
        return send(outv.at[n, y, h], outv.at[n, y, h], az_ss.at[0], az_rs.at[n], at(dz=2 * d))

    def aycopy(n, q):
        side = q % 2
        to, ss, rs = at(dy=1 - 2 * side), ay_ss.at[q // 2], ay_rs.at[n, q]
        block = outv.at[n, y] if q < 2 else outv.at[n, (ym, yp)[side], :, :, cols(side)]
        return send(block, block, ss, rs, to)

    def ag_f(n):
        wait(rz.at[n], rz_rs.at[n])
        total = zt[n, h]
        for d in range(3):
            total = total + rz[n, d].astype(F32)
        scale = lax.rsqrt(jnp.sum(total * total, axis=1, keepdims=True) + 1e-06)
        outv[n, y, h] = (total * scale).astype(BF16)
        for d in (2, 1, 3):
            azcopy(n, d).start()

    def ag_g(n):
        wait(rz.at[n], az_rs.at[n])
        for q in range(2):
            aycopy(n, q).start()

    def ag_h(n):
        for q in range(2):
            aycopy(n, q).wait_recv()
            aycopy(n, 2 + q).start()

    def ag_i(n):
        for q in range(2, 4):
            aycopy(n, q).wait_recv()

    def ccopy(n):
        d = n % 3 + 1
        if n < 3:
            return send(cnt.at[0], cnt_y.at[d - 1], c_ss.at[0], c_rs.at[0], at(dy=d))
        return send(cnt.at[1], cnt_z.at[d - 1], c_ss.at[1], c_rs.at[1], at(dz=2 * d))

    def cnt_a():
        rest, lanes = cacc[...], jnp.zeros((8, 1024), F32)
        ones = jnp.ones((8, 128), BF16)
        for _ in range(3):
            term = rest.astype(BF16)
            lanes += lax.dot_general(ones, term, (((1,), (1,)), ((), ())), preferred_element_type=F32)
            rest = rest - term.astype(F32)
        row = lax.broadcasted_iota(jnp.int32, (8, 128), 0)
        dense = jnp.zeros((8, 128), F32)
        for r in range(8):
            dense = jnp.where(row == r, lanes[:, r * 128 : (r + 1) * 128], dense)
        cnt[0] = dense
        for n in range(3):
            ccopy(n).start()

    def cnt_b():
        wait(cnt_y, c_rs.at[0])
        cnt[1] = cnt[0] + cnt_y[0] + cnt_y[1] + cnt_y[2]
        for n in range(3, 6):
            ccopy(n).start()

    def cnt_c():
        wait(cnt_z, c_rs.at[1])
        cnt_out[...] = cnt[1] + cnt_z[0] + cnt_z[1] + cnt_z[2]

    mm2(0, 0, 4)
    rs_a(0)
    mm2(1, 0, 4)
    rs_a(1)
    rs_b(0)
    mm2(2, 0, 4)
    rs_a(2)
    rs_b(1)
    rs_c(0)
    mm2(3, 0, 4)
    rs_a(3)
    rs_b(2)
    rs_c(1)
    ag_f(0)
    rs_b(3)
    rs_c(2)
    ag_f(1)
    rs_c(3)
    ag_g(0)
    ag_f(2)
    cnt_a()
    ag_g(1)
    ag_h(0)
    ag_f(3)
    ag_g(2)
    ag_h(1)
    cnt_b()
    ag_g(3)
    ag_h(2)
    ag_h(3)
    cnt_c()
    ag_i(0)
    ag_i(1)
    ag_i(2)
    ag_i(3)

    wait(pts.at[0, pl.ds(0, 2)], x_ss.at[0])
    wait(pts.at[0, 0], f_ss.at[0])
    wait(pts.at[0], z_ss.at[0])
    wait(pts.at[pl.ds(0, 2)], s_ss.at[0])
    wait(st_pair, sp_ss.at[0])
    wait(st_x, sx_ss.at[0])
    wait(st_z, sz_ss.at[0])
    wait(ry2, y2_ss.at[0])
    wait(rym, ym_ss.at[0])
    wait(rz, rz_ss.at[0])
    wait(rz, az_ss.at[0])
    wait(outv.at[pl.ds(0, 2)], ay_ss.at[0])
    wait(outv.at[0], ay_ss.at[1])
    wait(cnt_y, c_ss.at[0])
    wait(cnt_z, c_ss.at[1])


def on_device(points, centroids):
    dma = pltpu.SemaphoreType.DMA
    out, counts = pl.pallas_call(
        kernel,
        out_shape=(
            jax.ShapeDtypeStruct((4, 4, 4, 16, D), BF16),
            jax.ShapeDtypeStruct((8, 128), F32),
        ),
        in_specs=[pl.BlockSpec(memory_space=pl.ANY)] * 2,
        out_specs=[pl.BlockSpec(memory_space=pltpu.VMEM)] * 2,
        scratch_shapes=[
            pltpu.VMEM((4, 4, 2, 128, D), BF16),
            pltpu.VMEM((1024, D), BF16),
            pltpu.VMEM((4, 4, 1024, 256), F32),
            pltpu.VMEM((4, 4, 8, 128), F32),
            pltpu.VMEM((4, 4, 8, 128), F32),
            pltpu.VMEM((4, 4, 8, 128), F32),
            pltpu.VMEM((4, 2, 8, 128), F32),
            pltpu.VMEM((4, 2, 8, 128), F32),
            pltpu.VMEM((4, 2, 8, 128), F32),
            pltpu.VMEM((4, 8, 128), F32),
            pltpu.VMEM((4, 8, 128), F32),
            pltpu.VMEM((4, 3, 2, 8, 128), F32),
            pltpu.VMEM((4, 2, 4, 8, 128), F32),
            pltpu.VMEM((4, 4, 64, D), F32),
            pltpu.VMEM((1024, 128), F32),
            pltpu.VMEM((4, 4, 64, D), BF16),
            pltpu.VMEM((4, 2, 64, D // 2), BF16),
            pltpu.VMEM((4, 2, 64, D), BF16),
            pltpu.VMEM((4, 4, 16, D), F32),
            pltpu.VMEM((4, 4, 16, D), BF16),
            pltpu.VMEM((4, 3, 16, D), BF16),
            pltpu.VMEM((2, 8, 128), F32),
            pltpu.VMEM((3, 8, 128), F32),
            pltpu.VMEM((3, 8, 128), F32),
            dma((1,)), dma((NP, 2)), dma((1,)), dma((NP, 2)), dma((1,)), dma((4,)), dma((1,)), dma((8,)),
            dma((1,)), dma((4,)), dma((1,)), dma((4,)), dma((1,)), dma((4,)), pltpu.SemaphoreType.REGULAR,
            dma((1,)), dma((4, 2)), dma((1,)), dma((4,)), dma((1,)), dma((4,)),
            dma((1,)), dma((4,)), dma((2,)), dma((4, 4)), dma((2,)), dma((2,)), dma((2,)),
        ],
        compiler_params=pltpu.CompilerParams(
            collective_id=0, has_side_effects=True, vmem_limit_bytes=51 << 20
        ),
        cost_estimate=pl.CostEstimate(
            flops=4 * 4096 * 1024 * D, bytes_accessed=4 << 20, transcendentals=4096 * 1024
        ),
    )(points.reshape(2, 128, D), centroids)
    return out.reshape(1024, D), counts.reshape(1024)


def solution(mesh):
    placed = (P(("wide", "narrow"), None), P("narrow", None))
    return jax.shard_map(
        on_device,
        mesh=mesh,
        in_specs=placed,
        out_specs=(P("narrow", None), P("narrow")),
        check_vma=False,
    )
```

```python
import functools

import jax
import jax.numpy as jnp
from jax import lax
from jax.experimental import pallas as pl
from jax.experimental.pallas import tpu as pltpu
from jax.sharding import PartitionSpec as P

MESH = pl.DeviceIdType.MESH
F32 = jnp.float32
BF16 = jnp.bfloat16
D = 768
NP = 4
R = 128 // NP
KB = 256
RATE = 60.0 * 1.4426950408889634


def kernel(
    pts_in, cen_in, outv, cnt_out,
    pts, cen, e, m_tile, t_tile, s_tile, st_one, st_pair, st_chip, st_up, st_down, st_x, st_z,
    acc, cacc, yb, ry2, rym, zt, zb, rz, cnt, cnt_y, cnt_z,
    x_ss, x_rs, f_ss, f_rs, z_ss, z_rs, s_ss, s_rs, sp_ss, sp_rs, sx_ss, sx_rs, sz_ss, sz_rs, far,
    y2_ss, y2_rs, ym_ss, ym_rs, rz_ss, rz_rs, az_ss, az_rs, ay_ss, ay_rs, c_ss, c_rs, io_sem,
):
    wide, narrow = lax.axis_index("wide"), lax.axis_index("narrow")
    h, y = wide // 4, wide % 4
    zl, x, c = narrow // 8, (narrow // 2) % 4, narrow % 2
    z = 2 * h + zl
    xm, xp, x2 = (x + 3) % 4, (x + 1) % 4, (x + 2) % 4
    ym, yp, y2 = (y + 3) % 4, (y + 1) % 4, (y + 2) % 4

    def at(dx=0, dy=0, dz=0, dc=0):
        zz = (z + dz + 8) % 8
        return (
            (zz // 2) * 4 + (y + dy + 4) % 4,
            (zz % 2) * 8 + ((x + dx + 4) % 4) * 2 + (c + dc) % 2,
        )

    def send(src, dst, ss, rs, device):
        return pltpu.make_async_remote_copy(
            src_ref=src, dst_ref=dst, send_sem=ss, recv_sem=rs, device_id=device, device_id_type=MESH
        )

    def wait(ref, sem):
        send(ref, ref, sem, sem, at(dc=1)).wait_recv()

    cen_copy = pltpu.make_async_copy(cen_in, cen, io_sem.at[0])
    local = pltpu.make_async_copy(pts_in, pts.at[x, pl.ds(0, 2), c], io_sem.at[1])
    cen_copy.start()
    local.start()

    partners = [at(dc=1), at(dx=1), at(dx=-1), at(dy=1), at(dy=-1), at(dz=1), at(dz=-1)]
    barrier = pltpu.get_barrier_semaphore()
    for device in partners:
        pl.semaphore_signal(barrier, inc=1, device_id=device, device_id_type=MESH)
    pl.semaphore_wait(barrier, len(partners))

    sources = (x, xm, xp, x2)

    def piece(p):
        return pl.ds(p * R, R)

    def xcopy(p, way):
        return send(
            pts_in.at[:, piece(p)], pts.at[x, pl.ds(0, 2), c, piece(p)],
            x_ss.at[0], x_rs.at[p, way], at(dx=1 - 2 * way),
        )

    def fcopy(p, way):
        block = pts.at[(xm, xp)[way], way, c, piece(p)]
        return send(block, block, f_ss.at[0], f_rs.at[p, way], at(dx=1 - 2 * way))

    def zpoints(p, way, k):
        o = sources[k]
        src = pts_in.at[way, piece(p)] if k == 0 else pts.at[o, way, c, piece(p)]
        return send(src, pts.at[o, 2 + way, c, piece(p)], z_ss.at[0], z_rs.at[k], at(dz=1 - 2 * way))

    def sib(k, p=None):
        o, g = sources[k % 4], 2 * (k // 4)
        rows = pl.ds(0, 128) if p is None else piece(p)
        dst = pts.at[o, pl.ds(g, 2), c, rows]
        return send(pts_in if k == 0 else dst, dst, s_ss.at[0], s_rs.at[k], at(dc=1))

    def sib_arrived(k):
        wait(pts.at[0, pl.ds(0, 2), 0], s_rs.at[k])

    def ev0():
        for p in range(NP):
            for way in range(2):
                xcopy(p, way).start()
                zpoints(p, way, 0).start()
        sib(0).start()

    def ev1(p):
        for way in range(2):
            xcopy(p, way).wait_recv()
        for way in range(2):
            fcopy(p, way).start()
            for k in (1, 2):
                zpoints(p, way, k).start()
        for k in (1, 2):
            sib(k, p).start()

    def ev2(p):
        for way in range(2):
            fcopy(p, way).wait_recv()
            zpoints(p, way, 3).start()
        sib(3, p).start()

    def ev3(k):
        wait(pts.at[0, pl.ds(2, 2), c], z_rs.at[k])
        sib(4 + k).start()

    def mm1(i, w):
        p = pts[i, pl.ds(2 * w, 2)].reshape(512, D)
        for k in range(4):
            l = lax.dot_general(
                cen[k * KB : (k + 1) * KB, :], p, (((1,), (1,)), ((), ())), preferred_element_type=F32
            )
            m = jnp.max(l, axis=0, keepdims=True)
            v = jnp.exp2((l - m) * RATE)
            t = jnp.sum(v, axis=0, keepdims=True)
            for q in range(2):
                g = 2 * w + q
                e[i, g, k * KB : (k + 1) * KB, :] = v[:, q * 256 : (q + 1) * 256]
                for j in range(2):
                    row = pl.ds(2 * ((g + (g + 1) // 2) % 4) + j, 1)
                    lanes = slice(q * 256 + j * 128, q * 256 + (j + 1) * 128)
                    m_tile[i, k, row, :] = m[:, lanes]
                    t_tile[i, k, row, :] = t[:, lanes]

    def merge(parts):
        m = functools.reduce(jnp.maximum, [a for a, _ in parts])
        return m, sum(t * jnp.exp2((a - m) * RATE) for a, t in parts)

    def pair_copy(i):
        return send(st_one.at[i], st_pair.at[i], sp_ss.at[0], sp_rs.at[i], at(dc=1))

    def st_a(i):
        m, t = merge([(m_tile[i, k], t_tile[i, k]) for k in range(4)])
        st_one[i, 0] = m
        st_one[i, 1] = t
        pair_copy(i).start()

    def st_b(i):
        pair_copy(i).wait_recv()
        m, t = merge([(st_one[i, 0], st_one[i, 1]), (st_pair[i, 0], st_pair[i, 1])])
        st_chip[i, 0] = m
        st_chip[i, 1] = t
        st_up[i] = jnp.concatenate([m[2:4], m[0:2], t[2:4], t[0:2]], axis=0)
        st_down[i] = jnp.concatenate([m[6:8], m[4:6], t[6:8], t[4:6]], axis=0)

    def st_x_send(i):
        for d in (2, 1, 3):
            send(st_chip.at[i], st_x.at[i, d - 1], sx_ss.at[0], sx_rs.at[i], at(dx=d)).start()

    def st_c(i):
        for d in (2, 1, 3, 0):
            send(st_up.at[i], st_z.at[i, 0, d], sz_ss.at[0], sz_rs.at[i], at(dx=d, dz=1)).start()
            send(st_down.at[i], st_z.at[i, 1, d], sz_ss.at[0], sz_rs.at[i], at(dx=d, dz=-1)).start()

    def st_d(i, carry):
        wait(st_x.at[i], sx_rs.at[i])
        wait(st_z.at[i], sz_rs.at[i])
        mine = merge([(st_chip[i, 0], st_chip[i, 1])] + [(st_x[i, d, 0], st_x[i, d, 1]) for d in range(3)])
        far_z = [[(st_z[i, w, d][:4], st_z[i, w, d][4:]) for d in range(4)] for w in (1, 0)]
        above, below = merge(far_z[0]), merge(far_z[1])
        other = [jnp.concatenate([a, b], axis=0) for a, b in zip(above, below)]
        m, t = merge([mine, tuple(other)])
        inv = 1.0 / t
        for k in range(4):
            s_tile[i, k] = jnp.exp2((m_tile[i, k] - m) * RATE) * inv
        return carry

    ev0()
    cen_copy.wait()
    local.wait()

    def step(t, carry):
        def before(n, *acts):
            @pl.when(t == n)
            def _():
                for act in acts:
                    act()

        def do(f, *a):
            return functools.partial(f, *a)

        before(0, do(sib_arrived, 0))
        before(1, do(ev1, 0), do(ev1, 1), do(ev3, 0), do(ev1, 2), do(sib_arrived, 4))
        before(2, do(st_a, x), do(ev1, 3), do(ev2, 0), do(sib_arrived, 1))
        before(3, do(ev2, 1), do(sib_arrived, 2), do(st_b, x), do(st_x_send, x))
        before(4, do(ev2, 2), do(ev2, 3), do(ev3, 1), do(ev3, 2), do(sib_arrived, 5))
        before(5, do(st_a, xm), do(sib_arrived, 6))
        before(6, do(st_a, xp), do(st_b, xm), do(st_x_send, xm), do(ev3, 3), do(sib_arrived, 3))
        before(7, do(st_b, xp), do(st_x_send, xp), do(st_c, x), do(st_c, xm), do(st_c, xp), do(sib_arrived, 7))
        j = t // 2
        mid = (j % 3 + 1) // 2
        off = mid * (3 - 2 * (t % 2)) + (1 - mid) * (2 * (j // 3))
        mm1((x + off) % 4, mid * (j - 1) + (1 - mid) * (t % 2))
        return carry

    lax.fori_loop(0, 8, step, 0)
    st_a(x2)
    st_b(x2)
    st_c(x2)
    st_x_send(x2)
    lax.fori_loop(0, 4, st_d, 0)
    for d in (2, -2):
        pl.semaphore_signal(far, inc=1, device_id=at(dz=d), device_id_type=MESH)

    def mm2(n):
        rows = pl.ds(pl.multiple_of(n * KB, KB), KB)

        cs = jnp.zeros((KB, 128), F32)
        resp = []
        for i in range(4):
            for g in range(4):
                for j in range(2):
                    row = 2 * ((g + (g + 1) // 2) % 4) + j
                    v = e[i, g, rows, j * 128 : (j + 1) * 128] * s_tile[i, n, row : row + 1, :]
                    cs = cs + v
                    resp.append(v.astype(BF16))
        cacc[rows, :] = cs
        acc[n] = jnp.dot(
            jnp.concatenate(resp, axis=1), pts[...].reshape(4096, D), preferred_element_type=F32
        ).reshape(4, 64, D)

    def cols(side):
        return pl.ds(side * (D // 2), D // 2)

    def ycopy(n, kind, side):
        to, near = at(dy=1 - 2 * side), (yp, ym)[side]
        if kind == 0:
            return send(yb.at[n, y2, :, cols(side)], ry2.at[n, side], y2_ss.at[0], y2_rs.at[n, side], to)
        part = cols(1 - side if kind == 1 else side)
        return send(yb.at[n, near, :, part], rym.at[n, side, :, part], ym_ss.at[0], ym_rs.at[n], to)

    def rs_a(n):
        yb[n] = acc[n].astype(BF16)
        for kind in range(2):
            for side in range(2):
                ycopy(n, kind, side).start()

    def rs_b(n):
        for side, near in ((0, yp), (1, ym)):
            ycopy(n, 0, side).wait_recv()
            part = cols(side)
            yb[n, near, :, part] = (acc[n, near, :, part] + ry2[n, side].astype(F32)).astype(BF16)
            ycopy(n, 2, side).start()

    def zcopy(n, d):
        return send(zb.at[n, (h + d) % 4], rz.at[n, d - 1], rz_ss.at[0], rz_rs.at[n], at(dz=2 * d))

    def rs_c(n):
        wait(rym.at[n], ym_rs.at[n])
        total = acc[n, y] + rym[n, 0].astype(F32) + rym[n, 1].astype(F32)
        zt[n] = total.reshape(4, 16, D)
        zb[n] = total.astype(BF16).reshape(4, 16, D)

        @pl.when(n == 0)
        def _():
            pl.semaphore_wait(far, 2)

        for d in (2, 1, 3):
            zcopy(n, d).start()

    def azcopy(n, d):
        return send(outv.at[n, y, h], outv.at[n, y, h], az_ss.at[0], az_rs.at[n], at(dz=2 * d))

    def aycopy(n, q):
        side = q % 2
        to, ss, rs = at(dy=1 - 2 * side), ay_ss.at[q // 2], ay_rs.at[n, q]
        block = outv.at[n, y] if q < 2 else outv.at[n, (ym, yp)[side], :, :, cols(side)]
        return send(block, block, ss, rs, to)

    def ag_f(n):
        wait(rz.at[n], rz_rs.at[n])
        total = zt[n, h]
        for d in range(3):
            total = total + rz[n, d].astype(F32)
        scale = lax.rsqrt(jnp.sum(total * total, axis=1, keepdims=True) + 1e-06)
        outv[n, y, h] = (total * scale).astype(BF16)
        for d in (2, 1, 3):
            azcopy(n, d).start()

    def ag_g(n):
        wait(rz.at[n], az_rs.at[n])
        for q in range(2):
            aycopy(n, q).start()

    def ag_h(n):
        for q in range(2):
            aycopy(n, q).wait_recv()
            aycopy(n, 2 + q).start()

    def ag_i(n):
        for q in range(2, 4):
            aycopy(n, q).wait_recv()

    def ccopy(n):
        d = n % 3 + 1
        if n < 3:
            return send(cnt.at[0], cnt_y.at[d - 1], c_ss.at[0], c_rs.at[0], at(dy=d))
        return send(cnt.at[1], cnt_z.at[d - 1], c_ss.at[1], c_rs.at[1], at(dz=2 * d))

    def cnt_a():
        rest, lanes = cacc[...], jnp.zeros((8, 1024), F32)
        ones = jnp.ones((8, 128), BF16)
        for _ in range(3):
            term = rest.astype(BF16)
            lanes += lax.dot_general(ones, term, (((1,), (1,)), ((), ())), preferred_element_type=F32)
            rest = rest - term.astype(F32)
        row = lax.broadcasted_iota(jnp.int32, (8, 128), 0)
        dense = jnp.zeros((8, 128), F32)
        for r in range(8):
            dense = jnp.where(row == r, lanes[:, r * 128 : (r + 1) * 128], dense)
        cnt[0] = dense
        for n in range(3):
            ccopy(n).start()

    def cnt_b():
        wait(cnt_y, c_rs.at[0])
        cnt[1] = cnt[0] + cnt_y[0] + cnt_y[1] + cnt_y[2]
        for n in range(3, 6):
            ccopy(n).start()

    def cnt_c():
        wait(cnt_z, c_rs.at[1])
        cnt_out[...] = cnt[1] + cnt_z[0] + cnt_z[1] + cnt_z[2]

    def wave(s, carry):
        def chunk(lag, *acts):
            @pl.when((s >= lag) & (s < lag + 4))
            def _():
                for act in acts:
                    act(s - lag)

        chunk(0, mm2, rs_a)
        chunk(4, ag_f)
        chunk(1, rs_b)
        chunk(2, rs_c)
        chunk(5, ag_g)
        pl.when(s == 6)(cnt_a)
        chunk(6, ag_h)
        pl.when(s == 7)(cnt_b)
        return carry

    lax.fori_loop(0, 10, wave, 0)
    cnt_c()
    for n in range(4):
        ag_i(n)

    wait(pts.at[0, pl.ds(0, 2)], x_ss.at[0])
    wait(pts.at[0, 0], f_ss.at[0])
    wait(pts.at[0], z_ss.at[0])
    wait(pts.at[pl.ds(0, 2)], s_ss.at[0])
    wait(st_pair, sp_ss.at[0])
    wait(st_x, sx_ss.at[0])
    wait(st_z, sz_ss.at[0])
    wait(ry2, y2_ss.at[0])
    wait(rym, ym_ss.at[0])
    wait(rz, rz_ss.at[0])
    wait(rz, az_ss.at[0])
    wait(outv.at[pl.ds(0, 2)], ay_ss.at[0])
    wait(outv.at[0], ay_ss.at[1])
    wait(cnt_y, c_ss.at[0])
    wait(cnt_z, c_ss.at[1])


def on_device(points, centroids):
    dma = pltpu.SemaphoreType.DMA
    out, counts = pl.pallas_call(
        kernel,
        out_shape=(
            jax.ShapeDtypeStruct((4, 4, 4, 16, D), BF16),
            jax.ShapeDtypeStruct((8, 128), F32),
        ),
        in_specs=[pl.BlockSpec(memory_space=pl.ANY)] * 2,
        out_specs=[pl.BlockSpec(memory_space=pltpu.VMEM)] * 2,
        scratch_shapes=[
            pltpu.VMEM((4, 4, 2, 128, D), BF16),
            pltpu.VMEM((1024, D), BF16),
            pltpu.VMEM((4, 4, 1024, 256), F32),
            pltpu.VMEM((4, 4, 8, 128), F32),
            pltpu.VMEM((4, 4, 8, 128), F32),
            pltpu.VMEM((4, 4, 8, 128), F32),
            pltpu.VMEM((4, 2, 8, 128), F32),
            pltpu.VMEM((4, 2, 8, 128), F32),
            pltpu.VMEM((4, 2, 8, 128), F32),
            pltpu.VMEM((4, 8, 128), F32),
            pltpu.VMEM((4, 8, 128), F32),
            pltpu.VMEM((4, 3, 2, 8, 128), F32),
            pltpu.VMEM((4, 2, 4, 8, 128), F32),
            pltpu.VMEM((4, 4, 64, D), F32),
            pltpu.VMEM((1024, 128), F32),
            pltpu.VMEM((4, 4, 64, D), BF16),
            pltpu.VMEM((4, 2, 64, D // 2), BF16),
            pltpu.VMEM((4, 2, 64, D), BF16),
            pltpu.VMEM((4, 4, 16, D), F32),
            pltpu.VMEM((4, 4, 16, D), BF16),
            pltpu.VMEM((4, 3, 16, D), BF16),
            pltpu.VMEM((2, 8, 128), F32),
            pltpu.VMEM((3, 8, 128), F32),
            pltpu.VMEM((3, 8, 128), F32),
            dma((1,)), dma((NP, 2)), dma((1,)), dma((NP, 2)), dma((1,)), dma((4,)), dma((1,)), dma((8,)),
            dma((1,)), dma((4,)), dma((1,)), dma((4,)), dma((1,)), dma((4,)), pltpu.SemaphoreType.REGULAR,
            dma((1,)), dma((4, 2)), dma((1,)), dma((4,)), dma((1,)), dma((4,)),
            dma((1,)), dma((4,)), dma((2,)), dma((4, 4)), dma((2,)), dma((2,)), dma((2,)),
        ],
        compiler_params=pltpu.CompilerParams(
            collective_id=0, has_side_effects=True, vmem_limit_bytes=51 << 20
        ),
        cost_estimate=pl.CostEstimate(
            flops=4 * 4096 * 1024 * D, bytes_accessed=4 << 20, transcendentals=4096 * 1024
        ),
    )(points.reshape(2, 128, D), centroids)
    return out.reshape(1024, D), counts.reshape(1024)


def solution(mesh):
    placed = (P(("wide", "narrow"), None), P("narrow", None))
    return jax.shard_map(
        on_device,
        mesh=mesh,
        in_specs=placed,
        out_specs=(P("narrow", None), P("narrow")),
        check_vma=False,
    )
```

```python
import functools

import jax
import jax.numpy as jnp
from jax import lax
from jax.experimental import pallas as pl
from jax.experimental.pallas import tpu as pltpu
from jax.sharding import PartitionSpec as P

MESH = pl.DeviceIdType.MESH
F32 = jnp.float32
BF16 = jnp.bfloat16
D = 768
NP = 4
R = 128 // NP
KB = 256
RATE = 60.0 * 1.4426950408889634


def kernel(
    pts_in, cen_in, outv, cnt_out,
    pts, cen, e, m_tile, t_tile, s_tile, st_one, st_pair, st_chip, st_up, st_down, st_x, st_z,
    acc, cacc, yb, ry2, rym, zt, zb, rz, cnt, cnt_y, cnt_z,
    x_ss, x_rs, f_ss, f_rs, z_ss, z_rs, s_ss, s_rs, sp_ss, sp_rs, sx_ss, sx_rs, sz_ss, sz_rs, far,
    y2_ss, y2_rs, ym_ss, ym_rs, rz_ss, rz_rs, az_ss, az_rs, ay_ss, ay_rs, c_ss, c_rs, io_sem,
):
    wide, narrow = lax.axis_index("wide"), lax.axis_index("narrow")
    h, y = lax.div(wide, 4), lax.rem(wide, 4)
    zl, x, c = lax.div(narrow, 8), lax.rem(lax.div(narrow, 2), 4), lax.rem(narrow, 2)
    z = 2 * h + zl
    xs = [x] + [lax.rem(x + d, 4) for d in range(1, 4)]
    ys = [y] + [lax.rem(y + d, 4) for d in range(1, 4)]
    zs = {d: lax.rem(z + d, 8) for d in (1, 2, 4, 6, 7)}
    bases = {d: (lax.div(a, 2) * 4, lax.rem(a, 2) * 8) for d, a in zs.items()}
    bases[0] = (h * 4, zl * 8)
    _, xp, x2, xm = xs
    _, yp, y2, ym = ys

    def at(dx=0, dy=0, dz=0, dc=0):
        wide_base, narrow_base = bases[dz % 8]
        return wide_base + ys[dy % 4], narrow_base + 2 * xs[dx % 4] + (1 - c if dc else c)

    def send(src, dst, ss, rs, device):
        return pltpu.make_async_remote_copy(
            src_ref=src, dst_ref=dst, send_sem=ss, recv_sem=rs, device_id=device, device_id_type=MESH
        )

    def wait(ref, sem):
        send(ref, ref, sem, sem, at(dc=1)).wait_recv()

    cen_copy = pltpu.make_async_copy(cen_in, cen, io_sem.at[0])
    local = pltpu.make_async_copy(pts_in, pts.at[x, pl.ds(0, 2), c], io_sem.at[1])
    cen_copy.start()
    local.start()

    partners = [at(dc=1), at(dx=1), at(dx=-1), at(dy=1), at(dy=-1), at(dz=1), at(dz=-1)]
    barrier = pltpu.get_barrier_semaphore()
    for device in partners:
        pl.semaphore_signal(barrier, inc=1, device_id=device, device_id_type=MESH)
    pl.semaphore_wait(barrier, len(partners))

    sources = (x, xm, xp, x2)

    def piece(p):
        return pl.ds(p * R, R)

    def xcopy(p, way):
        return send(
            pts_in.at[:, piece(p)], pts.at[x, pl.ds(0, 2), c, piece(p)],
            x_ss.at[0], x_rs.at[p, way], at(dx=1 - 2 * way),
        )

    def fcopy(p, way):
        block = pts.at[(xm, xp)[way], way, c, piece(p)]
        return send(block, block, f_ss.at[0], f_rs.at[p, way], at(dx=1 - 2 * way))

    def zpoints(p, way, k):
        o = sources[k]
        src = pts_in.at[way, piece(p)] if k == 0 else pts.at[o, way, c, piece(p)]
        return send(src, pts.at[o, 2 + way, c, piece(p)], z_ss.at[0], z_rs.at[k], at(dz=1 - 2 * way))

    def sib(k, p=None):
        o, g = sources[k % 4], 2 * (k // 4)
        rows = pl.ds(0, 128) if p is None else piece(p)
        dst = pts.at[o, pl.ds(g, 2), c, rows]
        return send(pts_in if k == 0 else dst, dst, s_ss.at[0], s_rs.at[k], at(dc=1))

    def sib_arrived(k):
        wait(pts.at[0, pl.ds(0, 2), 0], s_rs.at[k])

    def ev0():
        for p in range(NP):
            for way in range(2):
                xcopy(p, way).start()
                zpoints(p, way, 0).start()
        sib(0).start()

    def ev1(p):
        for way in range(2):
            xcopy(p, way).wait_recv()
        for way in range(2):
            fcopy(p, way).start()
            for k in (1, 2):
                zpoints(p, way, k).start()
        for k in (1, 2):
            sib(k, p).start()

    def ev2(p):
        for way in range(2):
            fcopy(p, way).wait_recv()
            zpoints(p, way, 3).start()
        sib(3, p).start()

    def ev3(k):
        wait(pts.at[0, pl.ds(2, 2), c], z_rs.at[k])
        sib(4 + k).start()

    def mm1(i, w):
        p = pts[i, pl.ds(2 * w, 2)].reshape(512, D)
        for k in range(4):
            l = lax.dot_general(
                cen[k * KB : (k + 1) * KB, :], p, (((1,), (1,)), ((), ())), preferred_element_type=F32
            )
            m = jnp.max(l, axis=0, keepdims=True)
            v = jnp.exp2((l - m) * RATE)
            t = jnp.sum(v, axis=0, keepdims=True)
            for q in range(2):
                g = 2 * w + q
                e[i, g, k * KB : (k + 1) * KB, :] = v[:, q * 256 : (q + 1) * 256]
                for j in range(2):
                    row = pl.ds(2 * ((g + (g + 1) // 2) % 4) + j, 1)
                    lanes = slice(q * 256 + j * 128, q * 256 + (j + 1) * 128)
                    m_tile[i, k, row, :] = m[:, lanes]
                    t_tile[i, k, row, :] = t[:, lanes]

    def merge(parts):
        m = functools.reduce(jnp.maximum, [a for a, _ in parts])
        return m, sum(t * jnp.exp2((a - m) * RATE) for a, t in parts)

    def pair_copy(i):
        return send(st_one.at[i], st_pair.at[i], sp_ss.at[0], sp_rs.at[i], at(dc=1))

    def st_a(i):
        m, t = merge([(m_tile[i, k], t_tile[i, k]) for k in range(4)])
        st_one[i, 0] = m
        st_one[i, 1] = t
        pair_copy(i).start()

    def st_b(i):
        pair_copy(i).wait_recv()
        m, t = merge([(st_one[i, 0], st_one[i, 1]), (st_pair[i, 0], st_pair[i, 1])])
        st_chip[i, 0] = m
        st_chip[i, 1] = t
        st_up[i] = jnp.concatenate([m[2:4], m[0:2], t[2:4], t[0:2]], axis=0)
        st_down[i] = jnp.concatenate([m[6:8], m[4:6], t[6:8], t[4:6]], axis=0)

    def st_x_send(i):
        for d in (2, 1, 3):
            send(st_chip.at[i], st_x.at[i, d - 1], sx_ss.at[0], sx_rs.at[i], at(dx=d)).start()

    def st_c(i):
        for d in (2, 1, 3, 0):
            send(st_up.at[i], st_z.at[i, 0, d], sz_ss.at[0], sz_rs.at[i], at(dx=d, dz=1)).start()
            send(st_down.at[i], st_z.at[i, 1, d], sz_ss.at[0], sz_rs.at[i], at(dx=d, dz=-1)).start()

    def st_d(i, carry):
        wait(st_x.at[i], sx_rs.at[i])
        wait(st_z.at[i], sz_rs.at[i])
        mine = merge([(st_chip[i, 0], st_chip[i, 1])] + [(st_x[i, d, 0], st_x[i, d, 1]) for d in range(3)])
        far_z = [[(st_z[i, w, d][:4], st_z[i, w, d][4:]) for d in range(4)] for w in (1, 0)]
        above, below = merge(far_z[0]), merge(far_z[1])
        other = [jnp.concatenate([a, b], axis=0) for a, b in zip(above, below)]
        m, t = merge([mine, tuple(other)])
        inv = 1.0 / t
        for k in range(4):
            s_tile[i, k] = jnp.exp2((m_tile[i, k] - m) * RATE) * inv
        return carry

    ev0()
    cen_copy.wait()
    local.wait()

    def step(t, carry):
        def before(n, *acts):
            @pl.when(t == n)
            def _():
                for act in acts:
                    act()

        def do(f, *a):
            return functools.partial(f, *a)

        before(0, do(sib_arrived, 0))
        before(1, do(ev1, 0), do(ev1, 1), do(ev3, 0), do(ev1, 2), do(sib_arrived, 4))
        before(2, do(st_a, x), do(ev1, 3), do(ev2, 0), do(sib_arrived, 1))
        before(3, do(ev2, 1), do(sib_arrived, 2), do(st_b, x), do(st_x_send, x))
        before(4, do(ev2, 2), do(ev2, 3), do(ev3, 1), do(ev3, 2), do(sib_arrived, 5))
        before(5, do(st_a, xm), do(sib_arrived, 6))
        before(6, do(st_a, xp), do(st_b, xm), do(st_x_send, xm), do(ev3, 3), do(sib_arrived, 3))
        before(7, do(st_b, xp), do(st_x_send, xp), do(st_c, x), do(st_c, xm), do(st_c, xp), do(sib_arrived, 7))
        j = t // 2
        mid = (j % 3 + 1) // 2
        off = mid * (3 - 2 * (t % 2)) + (1 - mid) * (2 * (j // 3))
        mm1(lax.rem(x + off, 4), mid * (j - 1) + (1 - mid) * (t % 2))
        return carry

    lax.fori_loop(0, 8, step, 0)
    st_a(x2)
    st_b(x2)
    st_c(x2)
    st_x_send(x2)
    lax.fori_loop(0, 4, st_d, 0)
    for d in (2, -2):
        pl.semaphore_signal(far, inc=1, device_id=at(dz=d), device_id_type=MESH)

    def mm2(n):
        rows = pl.ds(pl.multiple_of(n * KB, KB), KB)

        cs = jnp.zeros((KB, 128), F32)
        resp = []
        for i in range(4):
            for g in range(4):
                for j in range(2):
                    row = 2 * ((g + (g + 1) // 2) % 4) + j
                    v = e[i, g, rows, j * 128 : (j + 1) * 128] * s_tile[i, n, row : row + 1, :]
                    cs = cs + v
                    resp.append(v.astype(BF16))
        cacc[rows, :] = cs
        acc[n] = jnp.dot(
            jnp.concatenate(resp, axis=1), pts[...].reshape(4096, D), preferred_element_type=F32
        ).reshape(4, 64, D)

    def cols(side):
        return pl.ds(side * (D // 2), D // 2)

    def ycopy(n, kind, side):
        to, near = at(dy=1 - 2 * side), (yp, ym)[side]
        if kind == 0:
            return send(yb.at[n, y2, :, cols(side)], ry2.at[n, side], y2_ss.at[0], y2_rs.at[n, side], to)
        part = cols(1 - side if kind == 1 else side)
        return send(yb.at[n, near, :, part], rym.at[n, side, :, part], ym_ss.at[0], ym_rs.at[n], to)

    def rs_a(n):
        yb[n] = acc[n].astype(BF16)
        for kind in range(2):
            for side in range(2):
                ycopy(n, kind, side).start()

    def rs_b(n):
        for side, near in ((0, yp), (1, ym)):
            ycopy(n, 0, side).wait_recv()
            part = cols(side)
            yb[n, near, :, part] = (acc[n, near, :, part] + ry2[n, side].astype(F32)).astype(BF16)
            ycopy(n, 2, side).start()

    def zcopy(n, d):
        return send(zb.at[n, lax.rem(h + d, 4)], rz.at[n, d - 1], rz_ss.at[0], rz_rs.at[n], at(dz=2 * d))

    def rs_c(n):
        wait(rym.at[n], ym_rs.at[n])
        total = acc[n, y] + rym[n, 0].astype(F32) + rym[n, 1].astype(F32)
        zt[n] = total.reshape(4, 16, D)
        zb[n] = total.astype(BF16).reshape(4, 16, D)

        @pl.when(n == 0)
        def _():
            pl.semaphore_wait(far, 2)

        for d in (2, 1, 3):
            zcopy(n, d).start()

    def azcopy(n, d):
        return send(outv.at[n, y, h], outv.at[n, y, h], az_ss.at[0], az_rs.at[n], at(dz=2 * d))

    def aycopy(n, q):
        side, kind = q % 2, q // 2
        to, ss, rs = at(dy=1 - 2 * side), ay_ss.at[kind], ay_rs.at[n, q]
        part = cols(1 - side if kind == 2 else side)
        block = outv.at[n, (ym, yp)[side] if kind == 1 else y, :, :, part]
        return send(block, block, ss, rs, to)

    def ag_f(n):
        wait(rz.at[n], rz_rs.at[n])
        total = zt[n, h]
        for d in range(3):
            total = total + rz[n, d].astype(F32)
        scale = lax.rsqrt(jnp.sum(total * total, axis=1, keepdims=True) + 1e-06)
        outv[n, y, h] = (total * scale).astype(BF16)
        for d in (2, 1, 3):
            azcopy(n, d).start()

    def ag_g(n):
        wait(rz.at[n], az_rs.at[n])
        for q in (0, 1, 4, 5):
            aycopy(n, q).start()

    def ag_h(n):
        for q in range(2):
            aycopy(n, q).wait_recv()
            aycopy(n, 2 + q).start()

    def ag_i(n):
        for q in range(2, 6):
            aycopy(n, q).wait_recv()

    def ccopy(n):
        d = n % 3 + 1
        if n < 3:
            return send(cnt.at[0], cnt_y.at[d - 1], c_ss.at[0], c_rs.at[0], at(dy=d))
        return send(cnt.at[1], cnt_z.at[d - 1], c_ss.at[1], c_rs.at[1], at(dz=2 * d))

    def cnt_a():
        rest, lanes = cacc[...], jnp.zeros((8, 1024), F32)
        ones = jnp.ones((8, 128), BF16)
        for _ in range(3):
            term = rest.astype(BF16)
            lanes += lax.dot_general(ones, term, (((1,), (1,)), ((), ())), preferred_element_type=F32)
            rest = rest - term.astype(F32)
        row = lax.broadcasted_iota(jnp.int32, (8, 128), 0)
        dense = jnp.zeros((8, 128), F32)
        for r in range(8):
            dense = jnp.where(row == r, lanes[:, r * 128 : (r + 1) * 128], dense)
        cnt[0] = dense
        for n in range(3):
            ccopy(n).start()

    def cnt_b():
        wait(cnt_y, c_rs.at[0])
        cnt[1] = cnt[0] + cnt_y[0] + cnt_y[1] + cnt_y[2]
        for n in range(3, 6):
            ccopy(n).start()

    def cnt_c():
        wait(cnt_z, c_rs.at[1])
        cnt_out[...] = cnt[1] + cnt_z[0] + cnt_z[1] + cnt_z[2]

    def wave(s, carry):
        def chunk(lag, *acts):
            @pl.when((s >= lag) & (s < lag + 4))
            def _():
                for act in acts:
                    act(s - lag)

        chunk(0, mm2, rs_a)
        chunk(4, ag_f)
        chunk(1, rs_b)
        chunk(2, rs_c)
        chunk(5, ag_g)
        pl.when(s == 6)(cnt_a)
        chunk(6, ag_h)
        pl.when(s == 7)(cnt_b)
        return carry

    lax.fori_loop(0, 10, wave, 0)
    cnt_c()
    for n in range(4):
        ag_i(n)

    wait(pts.at[0, pl.ds(0, 2)], x_ss.at[0])
    wait(pts.at[0, 0], f_ss.at[0])
    wait(pts.at[0], z_ss.at[0])
    wait(pts.at[pl.ds(0, 2)], s_ss.at[0])
    wait(st_pair, sp_ss.at[0])
    wait(st_x, sx_ss.at[0])
    wait(st_z, sz_ss.at[0])
    wait(ry2, y2_ss.at[0])
    wait(rym, ym_ss.at[0])
    wait(rz, rz_ss.at[0])
    wait(rz, az_ss.at[0])
    for n in range(3):
        wait(outv.at[0], ay_ss.at[n])
    wait(cnt_y, c_ss.at[0])
    wait(cnt_z, c_ss.at[1])


def on_device(points, centroids):
    dma = pltpu.SemaphoreType.DMA
    out, counts = pl.pallas_call(
        kernel,
        out_shape=(
            jax.ShapeDtypeStruct((4, 4, 4, 16, D), BF16),
            jax.ShapeDtypeStruct((8, 128), F32),
        ),
        in_specs=[pl.BlockSpec(memory_space=pl.ANY)] * 2,
        out_specs=[pl.BlockSpec(memory_space=pltpu.VMEM)] * 2,
        scratch_shapes=[
            pltpu.VMEM((4, 4, 2, 128, D), BF16),
            pltpu.VMEM((1024, D), BF16),
            pltpu.VMEM((4, 4, 1024, 256), F32),
            pltpu.VMEM((4, 4, 8, 128), F32),
            pltpu.VMEM((4, 4, 8, 128), F32),
            pltpu.VMEM((4, 4, 8, 128), F32),
            pltpu.VMEM((4, 2, 8, 128), F32),
            pltpu.VMEM((4, 2, 8, 128), F32),
            pltpu.VMEM((4, 2, 8, 128), F32),
            pltpu.VMEM((4, 8, 128), F32),
            pltpu.VMEM((4, 8, 128), F32),
            pltpu.VMEM((4, 3, 2, 8, 128), F32),
            pltpu.VMEM((4, 2, 4, 8, 128), F32),
            pltpu.VMEM((4, 4, 64, D), F32),
            pltpu.VMEM((1024, 128), F32),
            pltpu.VMEM((4, 4, 64, D), BF16),
            pltpu.VMEM((4, 2, 64, D // 2), BF16),
            pltpu.VMEM((4, 2, 64, D), BF16),
            pltpu.VMEM((4, 4, 16, D), F32),
            pltpu.VMEM((4, 4, 16, D), BF16),
            pltpu.VMEM((4, 3, 16, D), BF16),
            pltpu.VMEM((2, 8, 128), F32),
            pltpu.VMEM((3, 8, 128), F32),
            pltpu.VMEM((3, 8, 128), F32),
            dma((1,)), dma((NP, 2)), dma((1,)), dma((NP, 2)), dma((1,)), dma((4,)), dma((1,)), dma((8,)),
            dma((1,)), dma((4,)), dma((1,)), dma((4,)), dma((1,)), dma((4,)), pltpu.SemaphoreType.REGULAR,
            dma((1,)), dma((4, 2)), dma((1,)), dma((4,)), dma((1,)), dma((4,)),
            dma((1,)), dma((4,)), dma((3,)), dma((4, 6)), dma((2,)), dma((2,)), dma((2,)),
        ],
        compiler_params=pltpu.CompilerParams(
            collective_id=0, has_side_effects=True, vmem_limit_bytes=51 << 20
        ),
        cost_estimate=pl.CostEstimate(
            flops=4 * 4096 * 1024 * D, bytes_accessed=4 << 20, transcendentals=4096 * 1024
        ),
    )(*(pltpu.with_memory_space_constraint(a, pltpu.HBM) for a in (points.reshape(2, 128, D), centroids)))
    return out.reshape(1024, D), counts.reshape(1024)


def solution(mesh):
    placed = (P(("wide", "narrow"), None), P("narrow", None))
    return jax.shard_map(
        on_device,
        mesh=mesh,
        in_specs=placed,
        out_specs=(P("narrow", None), P("narrow")),
        check_vma=False,
    )
```

```python
import functools

import jax
import jax.numpy as jnp
from jax import lax
from jax.experimental import pallas as pl
from jax.experimental.pallas import tpu as pltpu
from jax.sharding import PartitionSpec as P

MESH = pl.DeviceIdType.MESH
F32 = jnp.float32
BF16 = jnp.bfloat16
D = 768
NP = 4
R = 128 // NP
KB = 256
RATE = 60.0 * 1.4426950408889634


def kernel(
    pts_in, cen_in, outv, cnt_out,
    pts, cen, e, m_tile, t_tile, s_tile, st_one, st_pair, st_chip, st_up, st_down, st_x, st_z,
    acc, cacc, yb, ry2, rym, zt, zb, rz, cnt, cnt_y, cnt_z,
    x_ss, x_rs, f_ss, f_rs, z_ss, z_rs, s_ss, s_rs, sp_ss, sp_rs, sx_ss, sx_rs, sz_ss, sz_rs, far,
    y2_ss, y2_rs, ym_ss, ym_rs, rz_ss, rz_rs, az_ss, az_rs, ay_ss, ay_rs, c_ss, c_rs, io_sem,
):
    wide, narrow = lax.axis_index("wide"), lax.axis_index("narrow")
    h, y = lax.div(wide, 4), lax.rem(wide, 4)
    zl, x, c = lax.div(narrow, 8), lax.rem(lax.div(narrow, 2), 4), lax.rem(narrow, 2)
    z = 2 * h + zl
    xs = [x] + [lax.rem(x + d, 4) for d in range(1, 4)]
    ys = [y] + [lax.rem(y + d, 4) for d in range(1, 4)]
    zs = {d: lax.rem(z + d, 8) for d in (1, 2, 4, 6, 7)}
    bases = {d: (lax.div(a, 2) * 4, lax.rem(a, 2) * 8) for d, a in zs.items()}
    bases[0] = (h * 4, zl * 8)
    _, xp, x2, xm = xs
    _, yp, y2, ym = ys

    def at(dx=0, dy=0, dz=0, dc=0):
        wide_base, narrow_base = bases[dz % 8]
        return wide_base + ys[dy % 4], narrow_base + 2 * xs[dx % 4] + (1 - c if dc else c)

    def send(src, dst, ss, rs, device):
        return pltpu.make_async_remote_copy(
            src_ref=src, dst_ref=dst, send_sem=ss, recv_sem=rs, device_id=device, device_id_type=MESH
        )

    def wait(ref, sem):
        send(ref, ref, sem, sem, at(dc=1)).wait_recv()

    cen_copy = pltpu.make_async_copy(cen_in, cen, io_sem.at[0])
    local = pltpu.make_async_copy(pts_in, pts.at[x, pl.ds(0, 2), c], io_sem.at[1])
    cen_copy.start()
    local.start()

    partners = [at(dc=1), at(dx=1), at(dx=-1), at(dy=1), at(dy=-1), at(dz=1), at(dz=-1)]
    barrier = pltpu.get_barrier_semaphore()
    for device in partners:
        pl.semaphore_signal(barrier, inc=1, device_id=device, device_id_type=MESH)
    pl.semaphore_wait(barrier, len(partners))

    sources = (x, xm, xp, x2)

    def piece(p):
        return pl.ds(p * R, R)

    def xcopy(p, way):
        return send(
            pts_in.at[:, piece(p)], pts.at[x, pl.ds(0, 2), c, piece(p)],
            x_ss.at[0], x_rs.at[p, way], at(dx=1 - 2 * way),
        )

    def fcopy(p, way):
        block = pts.at[(xm, xp)[way], way, c, piece(p)]
        return send(block, block, f_ss.at[0], f_rs.at[p, way], at(dx=1 - 2 * way))

    def zpoints(p, way, k):
        o = sources[k]
        src = pts_in.at[way, piece(p)] if k == 0 else pts.at[o, way, c, piece(p)]
        return send(src, pts.at[o, 2 + way, c, piece(p)], z_ss.at[0], z_rs.at[k], at(dz=1 - 2 * way))

    def sib(k, p=None):
        o, g = sources[k % 4], 2 * (k // 4)
        rows = pl.ds(0, 128) if p is None else piece(p)
        dst = pts.at[o, pl.ds(g, 2), c, rows]
        return send(pts_in if k == 0 else dst, dst, s_ss.at[0], s_rs.at[k], at(dc=1))

    def sib_arrived(k):
        wait(pts.at[0, pl.ds(0, 2), 0], s_rs.at[k])

    def ev0():
        for p in range(NP):
            for way in range(2):
                xcopy(p, way).start()
                zpoints(p, way, 0).start()
        sib(0).start()

    def ev1(p):
        for way in range(2):
            xcopy(p, way).wait_recv()
        for k in (1, 2):
            for way in range(2):
                zpoints(p, way, k).start()
        for way in range(2):
            fcopy(p, way).start()
        for k in (1, 2):
            sib(k, p).start()

    def ev2(p):
        for way in range(2):
            fcopy(p, way).wait_recv()
            zpoints(p, way, 3).start()
        sib(3, p).start()

    def ev3(k):
        wait(pts.at[0, pl.ds(2, 2), c], z_rs.at[k])
        sib(4 + k).start()

    def mm1(i, w):
        p = pts[i, pl.ds(2 * w, 2)].reshape(512, D)
        for k in range(4):
            l = lax.dot_general(
                cen[k * KB : (k + 1) * KB, :], p, (((1,), (1,)), ((), ())), preferred_element_type=F32
            )
            m = jnp.max(l, axis=0, keepdims=True)
            v = jnp.exp2((l - m) * RATE)
            t = jnp.sum(v, axis=0, keepdims=True)
            for q in range(2):
                g = 2 * w + q
                e[i, g, k * KB : (k + 1) * KB, :] = v[:, q * 256 : (q + 1) * 256]
                for j in range(2):
                    row = pl.ds(2 * ((g + (g + 1) // 2) % 4) + j, 1)
                    lanes = slice(q * 256 + j * 128, q * 256 + (j + 1) * 128)
                    m_tile[i, k, row, :] = m[:, lanes]
                    t_tile[i, k, row, :] = t[:, lanes]

    def merge(parts):
        m = functools.reduce(jnp.maximum, [a for a, _ in parts])
        return m, sum(t * jnp.exp2((a - m) * RATE) for a, t in parts)

    def pair_copy(i):
        return send(st_one.at[i], st_pair.at[i], sp_ss.at[0], sp_rs.at[i], at(dc=1))

    def st_a(i):
        m, t = merge([(m_tile[i, k], t_tile[i, k]) for k in range(4)])
        st_one[i, 0] = m
        st_one[i, 1] = t
        pair_copy(i).start()

    def st_b(i):
        pair_copy(i).wait_recv()
        m, t = merge([(st_one[i, 0], st_one[i, 1]), (st_pair[i, 0], st_pair[i, 1])])
        st_chip[i, 0] = m
        st_chip[i, 1] = t
        st_up[i] = jnp.concatenate([m[2:4], m[0:2], t[2:4], t[0:2]], axis=0)
        st_down[i] = jnp.concatenate([m[6:8], m[4:6], t[6:8], t[4:6]], axis=0)

    def st_x_send(i):
        for d in (2, 1, 3):
            send(st_chip.at[i], st_x.at[i, d - 1], sx_ss.at[0], sx_rs.at[i], at(dx=d)).start()

    def st_c(i):
        for d in (2, 1, 3, 0):
            send(st_up.at[i], st_z.at[i, 0, d], sz_ss.at[0], sz_rs.at[i], at(dx=d, dz=1)).start()
            send(st_down.at[i], st_z.at[i, 1, d], sz_ss.at[0], sz_rs.at[i], at(dx=d, dz=-1)).start()

    def st_d(i, carry):
        wait(st_x.at[i], sx_rs.at[i])
        wait(st_z.at[i], sz_rs.at[i])
        mine = merge([(st_chip[i, 0], st_chip[i, 1])] + [(st_x[i, d, 0], st_x[i, d, 1]) for d in range(3)])
        far_z = [[(st_z[i, w, d][:4], st_z[i, w, d][4:]) for d in range(4)] for w in (1, 0)]
        above, below = merge(far_z[0]), merge(far_z[1])
        other = [jnp.concatenate([a, b], axis=0) for a, b in zip(above, below)]
        m, t = merge([mine, tuple(other)])
        inv = 1.0 / t
        for k in range(4):
            s_tile[i, k] = jnp.exp2((m_tile[i, k] - m) * RATE) * inv
        return carry

    ev0()
    cen_copy.wait()
    local.wait()

    def step(t, carry):
        def before(n, *acts):
            @pl.when(t == n)
            def _():
                for act in acts:
                    act()

        def do(f, *a):
            return functools.partial(f, *a)

        before(0, do(sib_arrived, 0))
        before(1, do(ev1, 0), do(ev1, 1), do(ev3, 0), do(ev1, 2), do(sib_arrived, 4))
        before(2, do(st_a, x), do(ev1, 3), do(ev2, 0), do(sib_arrived, 1))
        before(3, do(ev2, 1), do(sib_arrived, 2), do(st_b, x), do(st_x_send, x))
        before(4, do(ev2, 2), do(ev2, 3), do(ev3, 1), do(ev3, 2), do(sib_arrived, 5))
        before(5, do(st_a, xm), do(sib_arrived, 6))
        before(6, do(st_a, xp), do(st_b, xm), do(st_x_send, xm), do(ev3, 3), do(sib_arrived, 3))
        before(7, do(st_b, xp), do(st_x_send, xp), do(st_c, x), do(st_c, xm), do(st_c, xp), do(sib_arrived, 7))
        j = t // 2
        mid = (j % 3 + 1) // 2
        off = mid * (3 - 2 * (t % 2)) + (1 - mid) * (2 * (j // 3))
        mm1(lax.rem(x + off, 4), mid * (j - 1) + (1 - mid) * (t % 2))
        return carry

    lax.fori_loop(0, 8, step, 0)
    st_a(x2)
    st_b(x2)
    st_c(x2)
    st_x_send(x2)
    lax.fori_loop(0, 4, st_d, 0)
    for d in (2, -2):
        pl.semaphore_signal(far, inc=1, device_id=at(dz=d), device_id_type=MESH)

    def mm2(n):
        rows = pl.ds(pl.multiple_of(n * KB, KB), KB)

        cs = jnp.zeros((KB, 128), F32)
        resp = []
        for i in range(4):
            for g in range(4):
                for j in range(2):
                    row = 2 * ((g + (g + 1) // 2) % 4) + j
                    v = e[i, g, rows, j * 128 : (j + 1) * 128] * s_tile[i, n, row : row + 1, :]
                    cs = cs + v
                    resp.append(v.astype(BF16))
        cacc[rows, :] = cs
        acc[n] = jnp.dot(
            jnp.concatenate(resp, axis=1), pts[...].reshape(4096, D), preferred_element_type=F32
        ).reshape(4, 64, D)

    def cols(side):
        return pl.ds(side * (D // 2), D // 2)

    def ycopy(n, kind, side):
        to, near = at(dy=1 - 2 * side), (yp, ym)[side]
        if kind == 0:
            return send(yb.at[n, y2, :, cols(side)], ry2.at[n, side], y2_ss.at[0], y2_rs.at[n, side], to)
        part = cols(1 - side if kind == 1 else side)
        return send(yb.at[n, near, :, part], rym.at[n, side, :, part], ym_ss.at[0], ym_rs.at[n], to)

    def rs_a(n):
        yb[n, y2] = acc[n, y2].astype(BF16)
        for side in range(2):
            ycopy(n, 0, side).start()
        for side, near in ((0, yp), (1, ym)):
            yb[n, near] = acc[n, near].astype(BF16)
            ycopy(n, 1, side).start()

    def rs_b(n):
        for side, near in ((0, yp), (1, ym)):
            ycopy(n, 0, side).wait_recv()
            part = cols(side)
            yb[n, near, :, part] = (acc[n, near, :, part] + ry2[n, side].astype(F32)).astype(BF16)
            ycopy(n, 2, side).start()

    def zcopy(n, d):
        return send(zb.at[n, lax.rem(h + d, 4)], rz.at[n, d - 1], rz_ss.at[0], rz_rs.at[n], at(dz=2 * d))

    def rs_c(n):
        wait(rym.at[n], ym_rs.at[n])
        total = acc[n, y] + rym[n, 0].astype(F32) + rym[n, 1].astype(F32)
        zt[n] = total.reshape(4, 16, D)
        zb[n] = total.astype(BF16).reshape(4, 16, D)

        @pl.when(n == 0)
        def _():
            pl.semaphore_wait(far, 2)

        for d in (2, 1, 3):
            zcopy(n, d).start()

    def azcopy(n, d):
        return send(outv.at[n, y, h], outv.at[n, y, h], az_ss.at[0], az_rs.at[n], at(dz=2 * d))

    def aycopy(n, q):
        side, kind = q % 2, q // 2
        to, ss, rs = at(dy=1 - 2 * side), ay_ss.at[kind], ay_rs.at[n, q]
        part = cols(1 - side if kind == 2 else side)
        block = outv.at[n, (ym, yp)[side] if kind == 1 else y, :, :, part]
        return send(block, block, ss, rs, to)

    def ag_f(n):
        wait(rz.at[n], rz_rs.at[n])
        total = zt[n, h]
        for d in range(3):
            total = total + rz[n, d].astype(F32)
        scale = lax.rsqrt(jnp.sum(total * total, axis=1, keepdims=True) + 1e-06)
        outv[n, y, h] = (total * scale).astype(BF16)
        for d in (2, 1, 3):
            azcopy(n, d).start()

    def ag_g(n):
        wait(rz.at[n], az_rs.at[n])
        for q in (0, 1, 4, 5):
            aycopy(n, q).start()

    def ag_h(n):
        for q in range(2):
            aycopy(n, q).wait_recv()
            aycopy(n, 2 + q).start()

    def ag_i(n):
        for q in range(2, 6):
            aycopy(n, q).wait_recv()

    def ccopy(n):
        d = n % 3 + 1
        if n < 3:
            return send(cnt.at[0], cnt_y.at[d - 1], c_ss.at[0], c_rs.at[0], at(dy=d))
        return send(cnt.at[1], cnt_z.at[d - 1], c_ss.at[1], c_rs.at[1], at(dz=2 * d))

    def cnt_a():
        rest, lanes = cacc[...], jnp.zeros((8, 1024), F32)
        ones = jnp.ones((8, 128), BF16)
        for _ in range(3):
            term = rest.astype(BF16)
            lanes += lax.dot_general(ones, term, (((1,), (1,)), ((), ())), preferred_element_type=F32)
            rest = rest - term.astype(F32)
        row = lax.broadcasted_iota(jnp.int32, (8, 128), 0)
        dense = jnp.zeros((8, 128), F32)
        for r in range(8):
            dense = jnp.where(row == r, lanes[:, r * 128 : (r + 1) * 128], dense)
        cnt[0] = dense
        for n in range(3):
            ccopy(n).start()

    def cnt_b():
        wait(cnt_y, c_rs.at[0])
        cnt[1] = cnt[0] + cnt_y[0] + cnt_y[1] + cnt_y[2]
        for n in range(3, 6):
            ccopy(n).start()

    def cnt_c():
        wait(cnt_z, c_rs.at[1])
        cnt_out[...] = cnt[1] + cnt_z[0] + cnt_z[1] + cnt_z[2]

    def wave(s, carry):
        def chunk(lag, *acts):
            @pl.when((s >= lag) & (s < lag + 4))
            def _():
                for act in acts:
                    act(s - lag)

        chunk(0, mm2, rs_a)
        chunk(4, ag_f)
        chunk(1, rs_b)
        chunk(2, rs_c)
        chunk(5, ag_g)
        pl.when(s == 6)(cnt_a)
        chunk(6, ag_h)
        pl.when(s == 7)(cnt_b)
        return carry

    lax.fori_loop(0, 10, wave, 0)
    cnt_c()
    for n in range(4):
        ag_i(n)

    wait(pts.at[0, pl.ds(0, 2)], x_ss.at[0])
    wait(pts.at[0, 0], f_ss.at[0])
    wait(pts.at[0], z_ss.at[0])
    wait(pts.at[pl.ds(0, 2)], s_ss.at[0])
    wait(st_pair, sp_ss.at[0])
    wait(st_x, sx_ss.at[0])
    wait(st_z, sz_ss.at[0])
    wait(ry2, y2_ss.at[0])
    wait(rym, ym_ss.at[0])
    wait(rz, rz_ss.at[0])
    wait(rz, az_ss.at[0])
    for n in range(3):
        wait(outv.at[0], ay_ss.at[n])
    wait(cnt_y, c_ss.at[0])
    wait(cnt_z, c_ss.at[1])


def on_device(points, centroids):
    dma = pltpu.SemaphoreType.DMA
    out, counts = pl.pallas_call(
        kernel,
        out_shape=(
            jax.ShapeDtypeStruct((4, 4, 4, 16, D), BF16),
            jax.ShapeDtypeStruct((8, 128), F32),
        ),
        in_specs=[pl.BlockSpec(memory_space=pl.ANY)] * 2,
        out_specs=[pl.BlockSpec(memory_space=pltpu.VMEM)] * 2,
        scratch_shapes=[
            pltpu.VMEM((4, 4, 2, 128, D), BF16),
            pltpu.VMEM((1024, D), BF16),
            pltpu.VMEM((4, 4, 1024, 256), F32),
            pltpu.VMEM((4, 4, 8, 128), F32),
            pltpu.VMEM((4, 4, 8, 128), F32),
            pltpu.VMEM((4, 4, 8, 128), F32),
            pltpu.VMEM((4, 2, 8, 128), F32),
            pltpu.VMEM((4, 2, 8, 128), F32),
            pltpu.VMEM((4, 2, 8, 128), F32),
            pltpu.VMEM((4, 8, 128), F32),
            pltpu.VMEM((4, 8, 128), F32),
            pltpu.VMEM((4, 3, 2, 8, 128), F32),
            pltpu.VMEM((4, 2, 4, 8, 128), F32),
            pltpu.VMEM((4, 4, 64, D), F32),
            pltpu.VMEM((1024, 128), F32),
            pltpu.VMEM((4, 4, 64, D), BF16),
            pltpu.VMEM((4, 2, 64, D // 2), BF16),
            pltpu.VMEM((4, 2, 64, D), BF16),
            pltpu.VMEM((4, 4, 16, D), F32),
            pltpu.VMEM((4, 4, 16, D), BF16),
            pltpu.VMEM((4, 3, 16, D), BF16),
            pltpu.VMEM((2, 8, 128), F32),
            pltpu.VMEM((3, 8, 128), F32),
            pltpu.VMEM((3, 8, 128), F32),
            dma((1,)), dma((NP, 2)), dma((1,)), dma((NP, 2)), dma((1,)), dma((4,)), dma((1,)), dma((8,)),
            dma((1,)), dma((4,)), dma((1,)), dma((4,)), dma((1,)), dma((4,)), pltpu.SemaphoreType.REGULAR,
            dma((1,)), dma((4, 2)), dma((1,)), dma((4,)), dma((1,)), dma((4,)),
            dma((1,)), dma((4,)), dma((3,)), dma((4, 6)), dma((2,)), dma((2,)), dma((2,)),
        ],
        compiler_params=pltpu.CompilerParams(
            collective_id=0, has_side_effects=True, vmem_limit_bytes=51 << 20
        ),
        cost_estimate=pl.CostEstimate(
            flops=4 * 4096 * 1024 * D, bytes_accessed=4 << 20, transcendentals=4096 * 1024
        ),
    )(*(pltpu.with_memory_space_constraint(a, pltpu.HBM) for a in (points.reshape(2, 128, D), centroids)))
    return out.reshape(1024, D), counts.reshape(1024)


def solution(mesh):
    placed = (P(("wide", "narrow"), None), P("narrow", None))
    return jax.shard_map(
        on_device,
        mesh=mesh,
        in_specs=placed,
        out_specs=(P("narrow", None), P("narrow")),
        check_vma=False,
    )
```

```python
import functools

import jax
import jax.numpy as jnp
from jax import lax
from jax.experimental import pallas as pl
from jax.experimental.pallas import tpu as pltpu
from jax.sharding import PartitionSpec as P

MESH = pl.DeviceIdType.MESH
F32 = jnp.float32
BF16 = jnp.bfloat16
D = 768
NP = 4
R = 128 // NP
KB = 256
RATE = 60.0 * 1.4426950408889634


def kernel(
    pts_in, cen_in, outv, cnt_out,
    pts, cen, e, m_tile, t_tile, s_tile, st_one, st_pair, st_chip, st_up, st_down, st_x, st_z,
    acc, cacc, yb, ry2, rym, zt, zb, rz, cnt, cnt_y, cnt_z,
    x_ss, x_rs, f_ss, f_rs, z_ss, z_rs, s_ss, s_rs, sp_ss, sp_rs, sx_ss, sx_rs, sz_ss, sz_rs, far,
    y2_ss, y2_rs, ym_ss, ym_rs, rz_ss, rz_rs, az_ss, az_rs, ay_ss, ay_rs, c_ss, c_rs, io_sem,
):
    wide, narrow = lax.axis_index("wide"), lax.axis_index("narrow")
    h, y = lax.div(wide, 4), lax.rem(wide, 4)
    zl, x, c = lax.div(narrow, 8), lax.rem(lax.div(narrow, 2), 4), lax.rem(narrow, 2)
    z = 2 * h + zl
    xs = [x] + [lax.rem(x + d, 4) for d in range(1, 4)]
    ys = [y] + [lax.rem(y + d, 4) for d in range(1, 4)]
    zs = {d: lax.rem(z + d, 8) for d in (1, 2, 4, 6, 7)}
    bases = {d: (lax.div(a, 2) * 4, lax.rem(a, 2) * 8) for d, a in zs.items()}
    bases[0] = (h * 4, zl * 8)
    _, xp, x2, xm = xs
    _, yp, y2, ym = ys

    def at(dx=0, dy=0, dz=0, dc=0):
        wide_base, narrow_base = bases[dz % 8]
        return wide_base + ys[dy % 4], narrow_base + 2 * xs[dx % 4] + (1 - c if dc else c)

    def send(src, dst, ss, rs, device):
        return pltpu.make_async_remote_copy(
            src_ref=src, dst_ref=dst, send_sem=ss, recv_sem=rs, device_id=device, device_id_type=MESH
        )

    def wait(ref, sem):
        send(ref, ref, sem, sem, at(dc=1)).wait_recv()

    cen_copy = pltpu.make_async_copy(cen_in, cen, io_sem.at[0])
    local = pltpu.make_async_copy(pts_in, pts.at[x, pl.ds(0, 2), c], io_sem.at[1])
    cen_copy.start()
    local.start()

    partners = [at(dc=1), at(dx=1), at(dx=-1), at(dy=1), at(dy=-1), at(dz=1), at(dz=-1)]
    barrier = pltpu.get_barrier_semaphore()
    for device in partners:
        pl.semaphore_signal(barrier, inc=1, device_id=device, device_id_type=MESH)
    pl.semaphore_wait(barrier, len(partners))

    sources = (x, xm, xp, x2)

    def piece(p):
        return pl.ds(p * R, R)

    def xcopy(p, way):
        return send(
            pts_in.at[:, piece(p)], pts.at[x, pl.ds(0, 2), c, piece(p)],
            x_ss.at[0], x_rs.at[p, way], at(dx=1 - 2 * way),
        )

    def fcopy(p, way):
        block = pts.at[(xm, xp)[way], way, c, piece(p)]
        return send(block, block, f_ss.at[0], f_rs.at[p, way], at(dx=1 - 2 * way))

    def zpoints(p, way, k):
        o = sources[k]
        src = pts_in.at[way, piece(p)] if k == 0 else pts.at[o, way, c, piece(p)]
        return send(src, pts.at[o, 2 + way, c, piece(p)], z_ss.at[0], z_rs.at[k], at(dz=1 - 2 * way))

    def sib(k, p=None):
        o, g = sources[k % 4], 2 * (k // 4)
        rows = pl.ds(0, 128) if p is None else piece(p)
        dst = pts.at[o, pl.ds(g, 2), c, rows]
        return send(pts_in if k == 0 else dst, dst, s_ss.at[0], s_rs.at[k], at(dc=1))

    def sib_arrived(k):
        wait(pts.at[0, pl.ds(0, 2), 0], s_rs.at[k])

    def ev0():
        for p in range(NP):
            for way in range(2):
                xcopy(p, way).start()
                zpoints(p, way, 0).start()
        sib(0).start()

    def ev1(p):
        for way in range(2):
            xcopy(p, way).wait_recv()
        for way in range(2):
            fcopy(p, way).start()
            for k in (1, 2):
                zpoints(p, way, k).start()
        for k in (1, 2):
            sib(k, p).start()

    def ev2(p):
        for way in range(2):
            fcopy(p, way).wait_recv()
            zpoints(p, way, 3).start()
        sib(3, p).start()

    def ev3(k):
        wait(pts.at[0, pl.ds(2, 2), c], z_rs.at[k])
        sib(4 + k).start()

    def mm1(i, w):
        p = pts[i, pl.ds(2 * w, 2)].reshape(512, D)
        for k in range(4):
            l = lax.dot_general(
                cen[k * KB : (k + 1) * KB, :], p, (((1,), (1,)), ((), ())), preferred_element_type=F32
            )
            m = jnp.max(l, axis=0, keepdims=True)
            v = jnp.exp2((l - m) * RATE)
            t = jnp.sum(v, axis=0, keepdims=True)
            for q in range(2):
                g = 2 * w + q
                e[i, g, k * KB : (k + 1) * KB, :] = v[:, q * 256 : (q + 1) * 256]
                for j in range(2):
                    row = pl.ds(2 * ((g + (g + 1) // 2) % 4) + j, 1)
                    lanes = slice(q * 256 + j * 128, q * 256 + (j + 1) * 128)
                    m_tile[i, k, row, :] = m[:, lanes]
                    t_tile[i, k, row, :] = t[:, lanes]

    def merge(parts):
        m = functools.reduce(jnp.maximum, [a for a, _ in parts])
        return m, sum(t * jnp.exp2((a - m) * RATE) for a, t in parts)

    def pair_copy(i):
        return send(st_one.at[i], st_pair.at[i], sp_ss.at[0], sp_rs.at[i], at(dc=1))

    def st_a(i):
        m, t = merge([(m_tile[i, k], t_tile[i, k]) for k in range(4)])
        st_one[i, 0] = m
        st_one[i, 1] = t
        pair_copy(i).start()

    def st_b(i):
        pair_copy(i).wait_recv()
        m, t = merge([(st_one[i, 0], st_one[i, 1]), (st_pair[i, 0], st_pair[i, 1])])
        st_chip[i, 0] = m
        st_chip[i, 1] = t
        st_up[i] = jnp.concatenate([m[2:4], m[0:2], t[2:4], t[0:2]], axis=0)
        st_down[i] = jnp.concatenate([m[6:8], m[4:6], t[6:8], t[4:6]], axis=0)

    def st_x_send(i):
        for d in (2, 1, 3):
            send(st_chip.at[i], st_x.at[i, d - 1], sx_ss.at[0], sx_rs.at[i], at(dx=d)).start()

    def st_c(i):
        for d in (2, 1, 3, 0):
            send(st_up.at[i], st_z.at[i, 0, d], sz_ss.at[0], sz_rs.at[i], at(dx=d, dz=1)).start()
            send(st_down.at[i], st_z.at[i, 1, d], sz_ss.at[0], sz_rs.at[i], at(dx=d, dz=-1)).start()

    def st_d(i, carry):
        wait(st_x.at[i], sx_rs.at[i])
        wait(st_z.at[i], sz_rs.at[i])
        mine = merge([(st_chip[i, 0], st_chip[i, 1])] + [(st_x[i, d, 0], st_x[i, d, 1]) for d in range(3)])
        far_z = [[(st_z[i, w, d][:4], st_z[i, w, d][4:]) for d in range(4)] for w in (1, 0)]
        above, below = merge(far_z[0]), merge(far_z[1])
        other = [jnp.concatenate([a, b], axis=0) for a, b in zip(above, below)]
        m, t = merge([mine, tuple(other)])
        inv = 1.0 / t
        for k in range(4):
            s_tile[i, k] = jnp.exp2((m_tile[i, k] - m) * RATE) * inv
        return carry

    ev0()
    cen_copy.wait()
    local.wait()

    def step(t, carry):
        def before(n, *acts):
            @pl.when(t == n)
            def _():
                for act in acts:
                    act()

        def do(f, *a):
            return functools.partial(f, *a)

        before(0, do(sib_arrived, 0))
        before(1, do(ev1, 0), do(ev1, 1), do(ev3, 0), do(ev1, 2), do(sib_arrived, 4))
        before(2, do(st_a, x), do(ev1, 3), do(ev2, 0), do(sib_arrived, 1))
        before(3, do(ev2, 1), do(sib_arrived, 2), do(st_b, x), do(st_x_send, x))
        before(4, do(ev2, 2), do(ev2, 3), do(ev3, 1), do(ev3, 2), do(sib_arrived, 5))
        before(5, do(st_a, xm), do(sib_arrived, 6))
        before(6, do(st_a, xp), do(st_b, xm), do(st_x_send, xm), do(ev3, 3), do(sib_arrived, 3))
        before(7, do(st_b, xp), do(st_x_send, xp), do(st_c, x), do(st_c, xm), do(st_c, xp), do(sib_arrived, 7))
        j = t // 2
        mid = (j % 3 + 1) // 2
        off = mid * (3 - 2 * (t % 2)) + (1 - mid) * (2 * (j // 3))
        mm1(lax.rem(x + off, 4), mid * (j - 1) + (1 - mid) * (t % 2))
        return carry

    lax.fori_loop(0, 8, step, 0)
    st_a(x2)
    st_b(x2)
    st_c(x2)
    st_x_send(x2)
    lax.fori_loop(0, 4, st_d, 0)
    for d in (2, -2):
        pl.semaphore_signal(far, inc=1, device_id=at(dz=d), device_id_type=MESH)

    def mm2(n):
        rows = pl.ds(pl.multiple_of(n * KB, KB), KB)

        cs = jnp.zeros((KB, 128), F32)
        resp = []
        for i in range(4):
            for g in range(4):
                for j in range(2):
                    row = 2 * ((g + (g + 1) // 2) % 4) + j
                    v = e[i, g, rows, j * 128 : (j + 1) * 128] * s_tile[i, n, row : row + 1, :]
                    cs = cs + v
                    resp.append(v.astype(BF16))
        cacc[rows, :] = cs
        acc[n] = jnp.dot(
            jnp.concatenate(resp, axis=1), pts[...].reshape(4096, D), preferred_element_type=F32
        ).reshape(4, 64, D)

    def cols(side):
        return pl.ds(side * (D // 2), D // 2)

    def ycopy(n, kind, side):
        to, near = at(dy=1 - 2 * side), (yp, ym)[side]
        if kind == 0:
            return send(yb.at[n, y2, :, cols(side)], ry2.at[n, side], y2_ss.at[0], y2_rs.at[n, side], to)
        part = cols(1 - side if kind == 1 else side)
        return send(yb.at[n, near, :, part], rym.at[n, side, :, part], ym_ss.at[0], ym_rs.at[n], to)

    def rs_a(n):
        yb[n] = acc[n].astype(BF16)
        for kind in range(2):
            for side in range(2):
                ycopy(n, kind, side).start()

    def rs_b(n):
        for side, near in ((0, yp), (1, ym)):
            ycopy(n, 0, side).wait_recv()
            part = cols(side)
            yb[n, near, :, part] = (acc[n, near, :, part] + ry2[n, side].astype(F32)).astype(BF16)
            ycopy(n, 2, side).start()

    def zcopy(n, d):
        return send(zb.at[n, lax.rem(h + d, 4)], rz.at[n, d - 1], rz_ss.at[0], rz_rs.at[n], at(dz=2 * d))

    def rs_c(n):
        wait(rym.at[n], ym_rs.at[n])
        total = acc[n, y] + rym[n, 0].astype(F32) + rym[n, 1].astype(F32)
        zt[n] = total.reshape(4, 16, D)
        zb[n] = total.astype(BF16).reshape(4, 16, D)

        @pl.when(n == 0)
        def _():
            pl.semaphore_wait(far, 2)

        for d in (2, 1, 3):
            zcopy(n, d).start()

    def azcopy(n, d):
        return send(outv.at[n, y, h], outv.at[n, y, h], az_ss.at[0], az_rs.at[n], at(dz=2 * d))

    def aycopy(n, q):
        side, kind = q % 2, q // 2
        to, ss, rs = at(dy=1 - 2 * side), ay_ss.at[kind], ay_rs.at[n, q]
        part = cols(1 - side if kind == 2 else side)
        block = outv.at[n, (ym, yp)[side] if kind == 1 else y, :, :, part]
        return send(block, block, ss, rs, to)

    def ag_f(n):
        wait(rz.at[n], rz_rs.at[n])
        total = zt[n, h]
        for d in range(3):
            total = total + rz[n, d].astype(F32)
        scale = lax.rsqrt(jnp.sum(total * total, axis=1, keepdims=True) + 1e-06)
        outv[n, y, h] = (total * scale).astype(BF16)
        for d in (2, 1, 3):
            azcopy(n, d).start()

    def ag_g(n):
        wait(rz.at[n], az_rs.at[n])
        for q in (0, 1, 4, 5):
            aycopy(n, q).start()

    def ag_h(n):
        for q in range(2):
            aycopy(n, q).wait_recv()
            aycopy(n, 2 + q).start()

    def ag_i(n):
        for q in range(2, 6):
            aycopy(n, q).wait_recv()

    def ccopy(n):
        d = n % 3 + 1
        if n < 3:
            return send(cnt.at[0], cnt_y.at[d - 1], c_ss.at[0], c_rs.at[0], at(dy=d))
        return send(cnt.at[1], cnt_z.at[d - 1], c_ss.at[1], c_rs.at[1], at(dz=2 * d))

    def cnt_a():
        rest, lanes = cacc[...], jnp.zeros((8, 1024), F32)
        ones = jnp.ones((8, 128), BF16)
        for _ in range(3):
            term = rest.astype(BF16)
            lanes += lax.dot_general(ones, term, (((1,), (1,)), ((), ())), preferred_element_type=F32)
            rest = rest - term.astype(F32)
        row = lax.broadcasted_iota(jnp.int32, (8, 128), 0)
        dense = jnp.zeros((8, 128), F32)
        for r in range(8):
            dense = jnp.where(row == r, lanes[:, r * 128 : (r + 1) * 128], dense)
        cnt[0] = dense
        for n in range(3):
            ccopy(n).start()

    def cnt_b():
        wait(cnt_y, c_rs.at[0])
        cnt[1] = cnt[0] + cnt_y[0] + cnt_y[1] + cnt_y[2]
        for n in range(3, 6):
            ccopy(n).start()

    def cnt_c():
        wait(cnt_z, c_rs.at[1])
        cnt_out[...] = cnt[1] + cnt_z[0] + cnt_z[1] + cnt_z[2]

    def wave(s, carry):
        def chunk(lag, *acts):
            @pl.when((s >= lag) & (s < lag + 4))
            def _():
                for act in acts:
                    act(s - lag)

        chunk(0, mm2, rs_a)
        chunk(4, ag_f)
        chunk(1, rs_b)
        chunk(2, rs_c)
        chunk(5, ag_g)
        pl.when(s == 6)(cnt_a)
        chunk(7, ag_h)
        pl.when(s == 7)(cnt_b)
        return carry

    lax.fori_loop(0, 11, wave, 0)
    cnt_c()
    for n in range(4):
        ag_i(n)

    wait(pts.at[0, pl.ds(0, 2)], x_ss.at[0])
    wait(pts.at[0, 0], f_ss.at[0])
    wait(pts.at[0], z_ss.at[0])
    wait(pts.at[pl.ds(0, 2)], s_ss.at[0])
    wait(st_pair, sp_ss.at[0])
    wait(st_x, sx_ss.at[0])
    wait(st_z, sz_ss.at[0])
    wait(ry2, y2_ss.at[0])
    wait(rym, ym_ss.at[0])
    wait(rz, rz_ss.at[0])
    wait(rz, az_ss.at[0])
    for n in range(3):
        wait(outv.at[0], ay_ss.at[n])
    wait(cnt_y, c_ss.at[0])
    wait(cnt_z, c_ss.at[1])


def on_device(points, centroids):
    dma = pltpu.SemaphoreType.DMA
    out, counts = pl.pallas_call(
        kernel,
        out_shape=(
            jax.ShapeDtypeStruct((4, 4, 4, 16, D), BF16),
            jax.ShapeDtypeStruct((8, 128), F32),
        ),
        in_specs=[pl.BlockSpec(memory_space=pl.ANY)] * 2,
        out_specs=[pl.BlockSpec(memory_space=pltpu.VMEM)] * 2,
        scratch_shapes=[
            pltpu.VMEM((4, 4, 2, 128, D), BF16),
            pltpu.VMEM((1024, D), BF16),
            pltpu.VMEM((4, 4, 1024, 256), F32),
            pltpu.VMEM((4, 4, 8, 128), F32),
            pltpu.VMEM((4, 4, 8, 128), F32),
            pltpu.VMEM((4, 4, 8, 128), F32),
            pltpu.VMEM((4, 2, 8, 128), F32),
            pltpu.VMEM((4, 2, 8, 128), F32),
            pltpu.VMEM((4, 2, 8, 128), F32),
            pltpu.VMEM((4, 8, 128), F32),
            pltpu.VMEM((4, 8, 128), F32),
            pltpu.VMEM((4, 3, 2, 8, 128), F32),
            pltpu.VMEM((4, 2, 4, 8, 128), F32),
            pltpu.VMEM((4, 4, 64, D), F32),
            pltpu.VMEM((1024, 128), F32),
            pltpu.VMEM((4, 4, 64, D), BF16),
            pltpu.VMEM((4, 2, 64, D // 2), BF16),
            pltpu.VMEM((4, 2, 64, D), BF16),
            pltpu.VMEM((4, 4, 16, D), F32),
            pltpu.VMEM((4, 4, 16, D), BF16),
            pltpu.VMEM((4, 3, 16, D), BF16),
            pltpu.VMEM((2, 8, 128), F32),
            pltpu.VMEM((3, 8, 128), F32),
            pltpu.VMEM((3, 8, 128), F32),
            dma((1,)), dma((NP, 2)), dma((1,)), dma((NP, 2)), dma((1,)), dma((4,)), dma((1,)), dma((8,)),
            dma((1,)), dma((4,)), dma((1,)), dma((4,)), dma((1,)), dma((4,)), pltpu.SemaphoreType.REGULAR,
            dma((1,)), dma((4, 2)), dma((1,)), dma((4,)), dma((1,)), dma((4,)),
            dma((1,)), dma((4,)), dma((3,)), dma((4, 6)), dma((2,)), dma((2,)), dma((2,)),
        ],
        compiler_params=pltpu.CompilerParams(
            collective_id=0, has_side_effects=True, vmem_limit_bytes=51 << 20
        ),
        cost_estimate=pl.CostEstimate(
            flops=4 * 4096 * 1024 * D, bytes_accessed=4 << 20, transcendentals=4096 * 1024
        ),
    )(*(pltpu.with_memory_space_constraint(a, pltpu.HBM) for a in (points.reshape(2, 128, D), centroids)))
    return out.reshape(1024, D), counts.reshape(1024)


def solution(mesh):
    placed = (P(("wide", "narrow"), None), P("narrow", None))
    return jax.shard_map(
        on_device,
        mesh=mesh,
        in_specs=placed,
        out_specs=(P("narrow", None), P("narrow")),
        check_vma=False,
    )
```
